32 devices in a mesh: dp: 8 (over z, y), tensor: 4 (over x, core).
Axes of the slice: x: 2, y: 2, z: 4, core: 2. Of those that a mesh axis runs over, the one named last changes fastest.
Arguments:
- target: bfloat16 [8, 1024, 768], P('dp'), may hold values from -6 to 6
- memory: bfloat16 [8, 512, 768], P('dp'), may hold values from -6 to 6
- target_segments: int32 [8, 1024], P('dp'), may hold values from 0 to 3, as said below
- memory_segments: int32 [8, 512], P('dp'), may hold values from 0 to 3, as said below
- cotangent: bfloat16 [8, 1024, 768], P('dp'), may hold values from -6 to 6
- input_weights: float32 [6, 768, 768], P(None, 'dp', 'tensor'), may hold values from -0.5412659 to 0.5412659
- input_moment: float32 [6, 768, 768], P(None, 'dp', 'tensor'), may hold values from -0.00048828125 to 0.00048828125
- input_square: float32 [6, 768, 768], P(None, 'dp', 'tensor'), may hold values from 1.05963814e-10 to 4.2385526e-10
- output_weights: float32 [2, 768, 768], P(None, 'tensor', 'dp'), may hold values from -0.625 to 0.625
- output_moment: float32 [2, 768, 768], P(None, 'tensor', 'dp'), may hold values from -0.00048828125 to 0.00048828125
- output_square: float32 [2, 768, 768], P(None, 'tensor', 'dp'), may hold values from 1.05963814e-10 to 4.2385526e-10
- expand_weights: float32 [768, 3072], P('dp', 'tensor'), may hold values from -0.21875 to 0.21875
- expand_moment: float32 [768, 3072], P('dp', 'tensor'), may hold values from -0.00048828125 to 0.00048828125
- expand_square: float32 [768, 3072], P('dp', 'tensor'), may hold values from 1.05963814e-10 to 4.2385526e-10
- contract_weights: float32 [3072, 768], P('tensor', 'dp'), may hold values from -0.109375 to 0.109375
- contract_moment: float32 [3072, 768], P('tensor', 'dp'), may hold values from -0.00048828125 to 0.00048828125
- contract_square: float32 [3072, 768], P('tensor', 'dp'), may hold values from 1.05963814e-10 to 4.2385526e-10
- head_biases: float32 [4, 768], P(None, 'tensor'), may hold values from -4 to 4
- head_moment: float32 [4, 768], P(None, 'tensor'), may hold values from -0.00048828125 to 0.00048828125
- head_square: float32 [4, 768], P(None, 'tensor'), may hold values from 1.05963814e-10 to 4.2385526e-10
- hidden_biases: float32 [3072], P('tensor'), may hold values from -4 to 4
- hidden_moment: float32 [3072], P('tensor'), may hold values from -0.00048828125 to 0.00048828125
- hidden_square: float32 [3072], P('tensor'), may hold values from 1.05963814e-10 to 4.2385526e-10
- row_vectors: float32 [9, 768], replicated, may hold values from -2 to 3.5
- row_moment: float32 [9, 768], replicated, may hold values from -0.00048828125 to 0.00048828125
- row_square: float32 [9, 768], replicated, may hold values from 1.05963814e-10 to 4.2385526e-10
Outputs:
- output: bfloat16 [8, 1024, 768], P('dp')
- target_grad: float32 [8, 1024, 768], P('dp')
- memory_grad: float32 [8, 512, 768], P('dp')
- grad_norm: float32 [], replicated
- new_input_weights: float32 [6, 768, 768], P(None, 'dp', 'tensor')
- new_input_moment: float32 [6, 768, 768], P(None, 'dp', 'tensor')
- new_input_square: float32 [6, 768, 768], P(None, 'dp', 'tensor')
- input_copy: bfloat16 [6, 768, 768], P(None, 'dp', 'tensor')
- new_output_weights: float32 [2, 768, 768], P(None, 'tensor', 'dp')
- new_output_moment: float32 [2, 768, 768], P(None, 'tensor', 'dp')
- new_output_square: float32 [2, 768, 768], P(None, 'tensor', 'dp')
- output_copy: bfloat16 [2, 768, 768], P(None, 'tensor', 'dp')
- new_expand_weights: float32 [768, 3072], P('dp', 'tensor')
- new_expand_moment: float32 [768, 3072], P('dp', 'tensor')
- new_expand_square: float32 [768, 3072], P('dp', 'tensor')
- expand_copy: bfloat16 [768, 3072], P('dp', 'tensor')
- new_contract_weights: float32 [3072, 768], P('tensor', 'dp')
- new_contract_moment: float32 [3072, 768], P('tensor', 'dp')
- new_contract_square: float32 [3072, 768], P('tensor', 'dp')
- contract_copy: bfloat16 [3072, 768], P('tensor', 'dp')
- new_head_biases: float32 [4, 768], P(None, 'tensor')
- new_head_moment: float32 [4, 768], P(None, 'tensor')
- new_head_square: float32 [4, 768], P(None, 'tensor')
- new_hidden_biases: float32 [3072], P('tensor')
- new_hidden_moment: float32 [3072], P('tensor')
- new_hidden_square: float32 [3072], P('tensor')
- new_row_vectors: float32 [9, 768], replicated
- new_row_moment: float32 [9, 768], replicated
- new_row_square: float32 [9, 768], replicated
The draws below stay inside these ranges and needn't reach their ends.
Inputs may be any that keep to these rules, and one draw needn't show every extreme that they name: `target_segments`: every sequence holds 4 documents numbered in order from 0; each is nonempty in the target tokens and in the memory rows of that sequence. `memory_segments`: numbered like target_segments of the same sequence; each document nonempty.
All inputs are finite; a program needn't handle non-finite values.
Results may differ from the reference program's by a relative error of at most 0.024.
Values may be sent and summed in bfloat16 or wider, within the bound.
No kernel may reach another device: no remote copies, remote signals or barrier semaphores. Data moves between devices by JAX's collectives and lax.ppermute only.
A program may use at most 128 MiB of HBM per device.

```python
import math
import jax
import jax.numpy as jnp
from jax import lax

D = 768
HEADS = 12
HEAD_DIM = 64
FF = 3072
SEQ = 1024
MSEQ = 512
DOCS = 4
STEP = 10
BATCH = 8


def cut_segments(seed_key, seq_len):
    scores = jax.random.randint(seed_key, (BATCH, seq_len - 1), 0, 2 ** 20)
    scores = scores * seq_len + jnp.arange(seq_len - 1, dtype=jnp.int32)[None, :]
    cuts = jax.lax.top_k(scores, DOCS - 1)[1].astype(jnp.int32) + 1
    places = jnp.arange(seq_len, dtype=jnp.int32)
    return jnp.sum((places[None, :, None] >= cuts[:, None, :]).astype(jnp.int32), axis=-1).astype(jnp.int32)


def draw_target_segments(key, part):
    key = jax.random.fold_in(key, 11)
    return cut_segments(key, SEQ)


def draw_memory_segments(key, part):
    key = jax.random.fold_in(key, 12)
    return cut_segments(key, MSEQ)


def draw_input_weights(key, part):
    key = jax.random.fold_in(key, 21)
    column = jnp.arange(D, dtype=jnp.float32) / D
    slot_index = jnp.arange(6)
    base_draw = jnp.clip(jax.random.normal(key, (6, D, D), jnp.float32), -6.0, 6.0)
    rise_factor = 0.6 * 3.0 ** column
    factor = jnp.where(((slot_index == 2) | (slot_index == 5))[:, None, None], rise_factor[None, None, :], 1.0)
    return base_draw * factor / math.sqrt(D)


def draw_row_vectors(key, part):
    key = jax.random.fold_in(key, 31)
    first_key, second_key = jax.random.split(key)
    column = jnp.arange(D, dtype=jnp.float32) / D
    row_index = jnp.arange(9)
    is_gain = (row_index == 3) | (row_index == 5) | (row_index == 7)
    gains = 0.6 * 3.0 ** column[None, :] * jax.random.uniform(first_key, (9, D), jnp.float32, 0.8, 1.2)
    shifts = 0.3 * jnp.clip(jax.random.normal(second_key, (9, D), jnp.float32), -6.0, 6.0)
    return jnp.where(is_gain[:, None], gains, shifts)


def steps_of(stream_key, shape, shards, low, top_value):
    def one(dim, blocks):
        steps = jax.random.uniform(jax.random.fold_in(jax.random.fold_in(stream_key, 6), dim), (blocks,), jnp.float32, low / len(shards), top_value / len(shards))
        return jnp.repeat(jnp.exp(steps), shape[dim] // blocks).reshape((-1,) + (1,) * (len(shape) - dim - 1))

    loudness = one(*shards[0])
    for cut in shards[1:]:
        loudness = loudness * one(*cut)
    return loudness


def bell_draw(key, extent, scale, bound, cuts=(), kind=jnp.bfloat16):
    entries = jax.random.normal(key, extent, jnp.float32) * scale
    if len(cuts) > 0:
        entries = steps_of(key, extent, cuts, -0.22, 0.18) * entries
    return jnp.clip(entries, min=-bound, max=bound).astype(kind)


def setup_inputs(seed: int = 0) -> dict:
    seeds = jax.random.split(jax.random.key(seed), 27)
    return {
        "target": bell_draw(seeds[0], (BATCH, SEQ, D), 1.0, 6.0, ((0, 8),)),
        "memory": bell_draw(seeds[1], (BATCH, MSEQ, D), 1.0, 6.0, ((0, 8),)),
        "target_segments": draw_target_segments(jax.random.fold_in(seeds[26], 71), 0),
        "memory_segments": draw_memory_segments(jax.random.fold_in(seeds[26], 71), 0),
        "cotangent": bell_draw(seeds[4], (BATCH, SEQ, D), 1.0, 6.0, ((0, 8),)),
        "input_weights": draw_input_weights(jax.random.fold_in(seeds[26], 71), 0),
        "input_moment": bell_draw(seeds[6], (6, D, D), (0.11 / (8 * D * D + 2 * D * FF) ** 0.5), 0.00048828125, ((1, 8), (2, 4)), jnp.float32),
        "input_square": jnp.clip(jnp.exp(math.log(4.2385525644839106e-10) - 1.3862944 * jax.random.uniform(seeds[7], (6, D, D), jnp.float32) ** steps_of(seeds[7], (6, D, D), ((1, 8), (2, 4)), -0.2, 0.2)), 1.0596381411209777e-10, 4.2385525644839106e-10),
        "output_weights": bell_draw(seeds[8], (2, D, D), (D // 8) ** -0.5, 0.625, ((1, 4), (2, 8)), jnp.float32),
        "output_moment": bell_draw(seeds[9], (2, D, D), (0.11 / (8 * D * D + 2 * D * FF) ** 0.5), 0.00048828125, ((1, 4), (2, 8)), jnp.float32),
        "output_square": jnp.clip(jnp.exp(math.log(4.2385525644839106e-10) - 1.3862944 * jax.random.uniform(seeds[10], (2, D, D), jnp.float32) ** steps_of(seeds[10], (2, D, D), ((1, 4), (2, 8)), -0.2, 0.2)), 1.0596381411209777e-10, 4.2385525644839106e-10),
        "expand_weights": bell_draw(seeds[11], (D, FF), D ** -0.5, 0.21875, ((0, 8), (1, 4)), jnp.float32),
        "expand_moment": bell_draw(seeds[12], (D, FF), (0.11 / (8 * D * D + 2 * D * FF) ** 0.5), 0.00048828125, ((0, 8), (1, 4)), jnp.float32),
        "expand_square": jnp.clip(jnp.exp(math.log(4.2385525644839106e-10) - 1.3862944 * jax.random.uniform(seeds[13], (D, FF), jnp.float32) ** steps_of(seeds[13], (D, FF), ((0, 8), (1, 4)), -0.2, 0.2)), 1.0596381411209777e-10, 4.2385525644839106e-10),
        "contract_weights": bell_draw(seeds[14], (FF, D), FF ** -0.5, 0.109375, ((0, 4), (1, 8)), jnp.float32),
        "contract_moment": bell_draw(seeds[15], (FF, D), (0.11 / (8 * D * D + 2 * D * FF) ** 0.5), 0.00048828125, ((0, 4), (1, 8)), jnp.float32),
        "contract_square": jnp.clip(jnp.exp(math.log(4.2385525644839106e-10) - 1.3862944 * jax.random.uniform(seeds[16], (FF, D), jnp.float32) ** steps_of(seeds[16], (FF, D), ((0, 4), (1, 8)), -0.2, 0.2)), 1.0596381411209777e-10, 4.2385525644839106e-10),
        "head_biases": bell_draw(seeds[17], (4, D), 0.3, 4.0, ((1, 4),), jnp.float32),
        "head_moment": bell_draw(seeds[18], (4, D), (0.11 / (8 * D * D + 2 * D * FF) ** 0.5), 0.00048828125, ((1, 4),), jnp.float32),
        "head_square": jnp.clip(jnp.exp(math.log(4.2385525644839106e-10) - 1.3862944 * jax.random.uniform(seeds[19], (4, D), jnp.float32) ** steps_of(seeds[19], (4, D), ((1, 4),), -0.2, 0.2)), 1.0596381411209777e-10, 4.2385525644839106e-10),
        "hidden_biases": bell_draw(seeds[20], (FF,), 0.3, 4.0, ((0, 4),), jnp.float32),
        "hidden_moment": bell_draw(seeds[21], (FF,), (0.11 / (8 * D * D + 2 * D * FF) ** 0.5), 0.00048828125, ((0, 4),), jnp.float32),
        "hidden_square": jnp.clip(jnp.exp(math.log(4.2385525644839106e-10) - 1.3862944 * jax.random.uniform(seeds[22], (FF,), jnp.float32) ** steps_of(seeds[22], (FF,), ((0, 4),), -0.2, 0.2)), 1.0596381411209777e-10, 4.2385525644839106e-10),
        "row_vectors": draw_row_vectors(jax.random.fold_in(seeds[26], 71), 0),
        "row_moment": bell_draw(seeds[24], (9, D), (0.11 / (8 * D * D + 2 * D * FF) ** 0.5), 0.00048828125, (), jnp.float32),
        "row_square": jnp.clip(jnp.exp(jax.random.uniform(seeds[25], (9, D), jnp.float32, math.log(1.0596381411209777e-10), math.log(4.2385525644839106e-10))), 1.0596381411209777e-10, 4.2385525644839106e-10),
    }


@jax.custom_vjp
def low(v):
    return lax.optimization_barrier(v.astype(jnp.bfloat16)).astype(jnp.float32)

@jax.custom_vjp
def low_back(v):
    return v

def low_keep(v):
    return (low(v), None)

def low_pass(kept, grad):
    return (grad,)

def back_keep(v):
    return (v, None)

def back_low(kept, grad):
    return (low(grad),)
low.defvjp(low_keep, low_pass)
low_back.defvjp(back_keep, back_low)
NORM_EPS = 1e-05
MASKED = -1e+30
BETA_ONE = 0.9
BETA_TWO = 0.999
RATE_MATRIX = 0.06
RATE_VECTOR = 0.5
DECAY = 0.01
ADAM_EPS = 1e-08
MAX_NORM = 1.0
HIGHEST = lax.Precision.HIGHEST

def product(left, right):
    return jnp.dot(left, right, precision=HIGHEST, preferred_element_type=jnp.float32)

def layer_norm(values, gain, shift):
    center = lax.optimization_barrier(jnp.mean(values, axis=-1, keepdims=True))
    centered = values - center
    spread = lax.optimization_barrier(jnp.mean(centered * centered, axis=-1, keepdims=True))
    return centered * lax.rsqrt(spread + NORM_EPS) * gain + shift

def gelu_exact(values):
    return 0.5 * values * (1.0 + lax.erf(values * 0.7071067811865476))

def attend(queries, key_rows, value_rows, allowed):
    query_heads = queries.reshape(queries.shape[0], HEADS, HEAD_DIM)
    key_heads = key_rows.reshape(key_rows.shape[0], HEADS, HEAD_DIM)
    value_heads = value_rows.reshape(value_rows.shape[0], HEADS, HEAD_DIM)
    scores = low_back(jnp.einsum('qhd,khd->hqk', query_heads, key_heads, precision=HIGHEST))
    scores = jnp.where(allowed[None], scores, MASKED)
    row_top = lax.optimization_barrier(jnp.max(scores, axis=-1, keepdims=True))
    exponent = jnp.exp(scores - row_top)
    weights = low(exponent / lax.optimization_barrier(jnp.sum(exponent, axis=-1, keepdims=True)))
    mixture = jnp.einsum('hqk,khd->qhd', weights, value_heads, precision=HIGHEST)
    return low(low_back(mixture.reshape(queries.shape[0], HEADS * HEAD_DIM)))

def forward(target_rows, memory_rows, target_seg, memory_seg, params):
    input_w, output_w, expand_w, contract_w, head_b, hidden_b, row_v = params
    in_low = low(input_w)
    out_low = low(output_w)
    expand_low = low(expand_w)
    contract_low = low(contract_w)
    rows_low = low(target_rows)
    queries = low(low_back((product(rows_low, in_low[0]) + head_b[0]) * 0.125))
    key_rows = low(low_back(product(rows_low, in_low[1])))
    value_rows = low(low_back(product(rows_low, in_low[2]) + head_b[1]))
    position = jnp.arange(SEQ)
    causal = (position[None, :] <= position[:, None]) & (target_seg[:, None] == target_seg[None, :])
    self_mixed = attend(queries, key_rows, value_rows, causal)
    self_branch = low_back(product(self_mixed, out_low[0]) + row_v[0])
    first = layer_norm(target_rows + self_branch, row_v[3], row_v[4])
    first_low = low(first)
    memory_low = low(memory_rows)
    cross_queries = low(low_back((product(first_low, in_low[3]) + head_b[2]) * 0.125))
    cross_keys = low(low_back(product(memory_low, in_low[4])))
    cross_values = low(low_back(product(memory_low, in_low[5]) + head_b[3]))
    linked = target_seg[:, None] == memory_seg[None, :]
    cross_mixed = attend(cross_queries, cross_keys, cross_values, linked)
    cross_branch = low_back(product(cross_mixed, out_low[1]) + row_v[1])
    second = layer_norm(first + cross_branch, row_v[5], row_v[6])
    second_low = low(second)
    hidden_pre = low_back(product(second_low, expand_low) + hidden_b)
    hidden = low(gelu_exact(hidden_pre))
    ffn_branch = low_back(product(hidden, contract_low) + row_v[2])
    return layer_norm(second + ffn_branch, row_v[7], row_v[8])

def adam(weight, gradient, moment, square, rate, clip_scale):
    clipped = gradient * clip_scale
    new_moment = BETA_ONE * moment + (1.0 - BETA_ONE) * clipped
    new_square = BETA_TWO * square + (1.0 - BETA_TWO) * clipped * clipped
    fixed_moment = new_moment / (1.0 - BETA_ONE ** STEP)
    fixed_square = new_square / (1.0 - BETA_TWO ** STEP)
    new_weight = weight - rate * (fixed_moment / (jnp.sqrt(fixed_square) + ADAM_EPS) + DECAY * weight)
    return (new_weight, new_moment, new_square)

def reference(target, memory, target_segments, memory_segments, cotangent, input_weights, input_moment, input_square, output_weights, output_moment, output_square, expand_weights, expand_moment, expand_square, contract_weights, contract_moment, contract_square, head_biases, head_moment, head_square, hidden_biases, hidden_moment, hidden_square, row_vectors, row_moment, row_square):
    params = (input_weights, output_weights, expand_weights, contract_weights, head_biases, hidden_biases, row_vectors)

    def one_sequence(running, item):
        rows_in, memory_in, row_seg, memory_seg, back_in = item

        def run(row_values, memory_values, weights):
            return forward(row_values, memory_values, row_seg, memory_seg, weights)
        result, pull = jax.vjp(run, rows_in.astype(jnp.float32), memory_in.astype(jnp.float32), params)
        grad_rows, grad_memory, grad_params = pull(back_in.astype(jnp.float32))
        running = jax.tree.map(lambda first_sum, second_sum: first_sum + second_sum, running, grad_params)
        return (running, (result.astype(jnp.bfloat16), grad_rows, grad_memory))
    start_grads = jax.tree.map(jnp.zeros_like, params)
    grads, (output, target_grad, memory_grad) = lax.scan(one_sequence, start_grads, (target, memory, target_segments, memory_segments, cotangent))
    squares = sum((jnp.sum(leaf_grad * leaf_grad) for leaf_grad in grads))
    grad_norm = jnp.sqrt(squares)
    clip_scale = jnp.minimum(1.0, MAX_NORM / (grad_norm + 1e-06))
    in_new = adam(input_weights, grads[0], input_moment, input_square, RATE_MATRIX, clip_scale)
    out_new = adam(output_weights, grads[1], output_moment, output_square, RATE_MATRIX, clip_scale)
    expand_new = adam(expand_weights, grads[2], expand_moment, expand_square, RATE_MATRIX, clip_scale)
    contract_new = adam(contract_weights, grads[3], contract_moment, contract_square, RATE_MATRIX, clip_scale)
    head_new = adam(head_biases, grads[4], head_moment, head_square, RATE_VECTOR, clip_scale)
    hidden_new = adam(hidden_biases, grads[5], hidden_moment, hidden_square, RATE_VECTOR, clip_scale)
    row_new = adam(row_vectors, grads[6], row_moment, row_square, RATE_VECTOR, clip_scale)
    return (output, target_grad, memory_grad, grad_norm, in_new[0], in_new[1], in_new[2], in_new[0].astype(jnp.bfloat16), out_new[0], out_new[1], out_new[2], out_new[0].astype(jnp.bfloat16), expand_new[0], expand_new[1], expand_new[2], expand_new[0].astype(jnp.bfloat16), contract_new[0], contract_new[1], contract_new[2], contract_new[0].astype(jnp.bfloat16), head_new[0], head_new[1], head_new[2], hidden_new[0], hidden_new[1], hidden_new[2], row_new[0], row_new[1], row_new[2])
```

```python
from functools import partial

import jax
import jax.numpy as jnp
from jax import lax
from jax.experimental import pallas as pl
from jax.experimental.pallas import tpu as pltpu
from jax.sharding import PartitionSpec as P

HEAD_DIM = 64
STEP = 10
NORM_EPS = 1e-05
BETA_ONE = 0.9
BETA_TWO = 0.999
RATE_MATRIX = 0.06
RATE_VECTOR = 0.5
DECAY = 0.01
ADAM_EPS = 1e-08
MAX_NORM = 1.0
BIG = 1e30
LANES = 256
MIB = 2**20
COST = 1.0

BF = jnp.bfloat16
F32 = jnp.float32
SDS = jax.ShapeDtypeStruct


def nn(left, right):
    return jnp.dot(left, right, preferred_element_type=F32)


def nt(left, right):
    return lax.dot_general(left, right, (((1,), (1,)), ((), ())), preferred_element_type=F32)


def tn(left, right):
    return lax.dot_general(left, right, (((0,), (0,)), ((), ())), preferred_element_type=F32)


def iota(shape, dim):
    return lax.broadcasted_iota(jnp.int32, shape, dim)


class Late:
    def __init__(self, copy, buffer):
        self.copy, self.buffer, self.waited = copy, buffer, False

    def __call__(self):
        if not self.waited:
            self.copy.wait()
            self.waited = True
        return self.buffer


class Saved:
    def __init__(self, copy, buffer):
        self.copy, self.buffer, self.started = copy, buffer, False

    def __call__(self):
        return self.buffer

    def flush(self):
        self.copy.start()
        self.started = True


def call(body, ids, ins, late, outs, saved, scratch=(), flops=0, vmem=32, name=None):
    counts = [len(ins), len(late), len(outs), len(saved), len(late), len(saved), len(scratch)]

    def kernel(ids_ref, *refs):
        groups = []
        start = 0
        for number in counts:
            groups.append(refs[start : start + number])
            start += number
        in_refs, late_refs, out_refs, saved_refs, late_bufs, saved_bufs, extra = groups
        sems = refs[start] if late or saved else None
        lates = [
            Late(pltpu.make_async_copy(ref, buf, sems.at[i]), buf)
            for i, (ref, buf) in enumerate(zip(late_refs, late_bufs))
        ]
        for item in lates:
            item.copy.start()
        saves = [
            Saved(pltpu.make_async_copy(buf, ref, sems.at[len(late) + i]), buf)
            for i, (ref, buf) in enumerate(zip(saved_refs, saved_bufs))
        ]
        body(ids_ref, in_refs, lates, out_refs, saves, extra)
        for item in lates:
            item()
        for item in saves:
            if not item.started:
                item.flush()
        for item in saves:
            item.copy.wait()

    size = sum(a.size * a.dtype.itemsize for a in [*ins, *late])
    size += sum(o.size * o.dtype.itemsize for o in [*outs, *saved])
    vmem_spec = pl.BlockSpec(memory_space=pltpu.VMEM)
    hbm_spec = pl.BlockSpec(memory_space=pltpu.HBM)
    sems = [pltpu.SemaphoreType.DMA((len(late) + len(saved),))] if late or saved else []
    result = pl.pallas_call(
        kernel,
        out_shape=[*outs, *saved],
        in_specs=[pl.BlockSpec(memory_space=pltpu.SMEM)]
        + [vmem_spec] * len(ins)
        + [hbm_spec] * len(late),
        out_specs=[vmem_spec] * len(outs) + [hbm_spec] * len(saved),
        scratch_shapes=[pltpu.VMEM(a.shape, a.dtype) for a in [*late, *saved]]
        + list(scratch)
        + sems,
        compiler_params=pltpu.CompilerParams(vmem_limit_bytes=vmem * MIB),
        cost_estimate=pl.CostEstimate(
            flops=int(flops * COST), bytes_accessed=int(size * COST), transcendentals=0
        ),
        name=name,
    )(ids, *ins, *late)
    return result


def after(value, *others):
    if not others:
        return value
    return lax.optimization_barrier((value, *others))[0]


def block_start(index, rows, blocks, hop):
    if blocks == 1:
        return 0
    return pl.multiple_of(jnp.bitwise_xor(index, hop) * rows, rows)


def pieces(parts, place, pack):
    if len(parts) == 2:
        side = jnp.bitwise_and(place, 1)
        rows = parts[0].shape[2]
        for half, part in enumerate(parts):
            for level in range(4):
                index = 2 * level + jnp.bitwise_xor(side, half)
                yield part.at[level, pack], pl.multiple_of(index * rows, rows)
    else:
        for hop, part in enumerate(parts):
            block = part if pack is None else part.at[pack]
            rows = block.shape[0]
            yield block, block_start(place, rows, len(parts), hop)


def place_padded(parts, place, out, pack=None):
    width = parts[0].shape[-1] // 4
    for group in range(4):
        out[:, group * LANES + width : (group + 1) * LANES] = jnp.zeros(
            (out.shape[0], LANES - width), BF
        )
    for part, start in pieces(parts, place, pack):
        for group in range(4):
            out[pl.ds(start, part.shape[0]), group * LANES : group * LANES + width] = part[
                :, group * width : (group + 1) * width
            ]


def place_plain(parts, place, out, pack=None):
    for part, start in pieces(parts, place, pack):
        out[pl.ds(start, part.shape[0]), :] = part[...]


def normalize(values):
    center = jnp.mean(values, axis=-1, keepdims=True)
    centered = values - center
    spread = jnp.mean(centered * centered, axis=-1, keepdims=True)
    scale_row = lax.rsqrt(spread + NORM_EPS)
    return centered * scale_row, scale_row


def norm_back(grad_out, normed, scale_row, gain):
    scaled = grad_out * gain
    return scale_row * (
        scaled
        - jnp.mean(scaled, axis=-1, keepdims=True)
        - normed * jnp.mean(scaled * normed, axis=-1, keepdims=True)
    )


def col_sum(values):
    return jnp.sum(values, axis=0, keepdims=True)


def head_mask(rows, width, head):
    lane = iota((rows, LANES), 1)
    return (lane >= head * HEAD_DIM) & (lane < (head + 1) * HEAD_DIM)


def tag_queries(queries, seg, width):
    doc = iota(queries.shape, 1) - width
    tagged = (doc >= 0) & (doc < 4)
    return jnp.where(tagged, jnp.where(doc == seg, 0.0, -BIG), queries).astype(BF)


def tag_keys(keys, seg, width):
    doc = iota(keys.shape, 1) - width
    return jnp.where(doc == seg, 1.0, keys).astype(BF)


def attend(queries, keys, values, width, causal_from, mixed_out, logsum_out):
    rows = queries.shape[0]
    count = keys.shape[0]
    lane = iota((rows, LANES), 1)
    mixed = jnp.zeros((rows, LANES), F32)
    for head in range(width // HEAD_DIM):
        mask = head_mask(rows, width, head) | (lane >= width)
        scores = nt(jnp.where(mask, queries, jnp.zeros_like(queries)), keys)
        if causal_from is not None:
            ahead = iota((rows, rows), 1) <= iota((rows, rows), 0)
            last = jnp.where(ahead, scores[:, causal_from:], -BIG)
            if causal_from:
                scores = jnp.concatenate([scores[:, :causal_from], last], 1)
            else:
                scores = last
        top = jnp.max(scores, axis=1, keepdims=True)
        weights = jnp.exp(scores - top)
        total = jnp.sum(weights, axis=1, keepdims=True)
        mixed = mixed + nn(weights.astype(BF), values[head]) * (1.0 / total)
        logsum_out(head, (top + jnp.log(total)).reshape(1, rows))
    mixed_out(mixed.astype(BF))


def attend_back(queries, keys, values, keys_t, grad, mixed, logsum, width, causal_from, add_key, add_value):
    rows = queries.shape[0]
    lane = iota((rows, LANES), 1)
    along = (grad.astype(F32) * mixed.astype(F32)).T
    parts = []
    zero = jnp.zeros_like(queries)
    for head in range(width // HEAD_DIM):
        low, high = head * HEAD_DIM, (head + 1) * HEAD_DIM
        mask = head_mask(rows, width, head)
        own_query = jnp.where(mask, queries, zero)
        own_grad = jnp.where(mask, grad, zero)
        scores = nt(keys, jnp.where(lane >= width, queries, own_query))
        if causal_from is not None:
            ahead = iota((rows, rows), 0) <= iota((rows, rows), 1)
            last = jnp.where(ahead, scores[causal_from:, :], -BIG)
            if causal_from:
                scores = jnp.concatenate([scores[:causal_from, :], last], 0)
            else:
                scores = last
        weights = jnp.exp(scores - logsum(head))
        grad_weights = nt(values, own_grad)
        grad_scores = (weights * (grad_weights - col_sum(along[low:high]))).astype(BF)
        add_value(nn(weights.astype(BF), own_grad))
        add_key(nn(grad_scores, own_query))
        parts.append(nn(keys_t[low:high], grad_scores))
    parts.append(jnp.zeros((LANES - width, rows), F32))
    return jnp.concatenate(parts, 0).T


def split_values(values, width):
    rows = values.shape[0]
    zero = jnp.zeros((rows, LANES), BF)
    return [
        jnp.where(head_mask(rows, width, head), values, zero) for head in range(width // HEAD_DIM)
    ]


def transposed(values):
    return values.astype(F32).T.astype(BF)


def self_kernel(width, ids, ins, late, outs, saved, scratch):
    target, seg, bias = ins[:3]
    parts = ins[3:]
    keep_own, keep_x, send = outs
    place, rank = ids[0], ids[1]
    wide, state, lse_out = (item() for item in saved)
    q_out, k_out, v_out, mixed_out = (
        state.at[:, i * LANES : (i + 1) * LANES] for i in range(4)
    )
    place_padded(parts, place, wide)
    saved[0].flush()
    rows = target[...]
    length = rows.shape[0]
    block = length // 4
    segments = seg[...]
    q_out[...] = tag_queries((nn(rows, wide[:, :LANES]) + bias[0:1, :]) * 0.125, segments, width)
    k_out[...] = tag_keys(nn(rows, wide[:, LANES : 2 * LANES]), segments, width)
    v_out[...] = (nn(rows, wide[:, 2 * LANES : 3 * LANES]) + bias[1:2, :]).astype(BF)
    values = split_values(v_out[...], width)
    lse_out[...] = jnp.zeros_like(lse_out)
    for index in range(4):
        start, stop = index * block, (index + 1) * block

        def put_mixed(mixed):
            mixed_out[start:stop, :] = mixed

        def put_lse(head, row):
            lse_out[head : head + 1, start:stop] = row

        attend(
            q_out[start:stop, :],
            k_out[:stop, :],
            [value[:stop] for value in values],
            width,
            start,
            put_mixed,
            put_lse,
        )
    saved[1].flush()
    saved[2].flush()
    back = wide[:, 3 * LANES :]
    for hop in (3, 1, 2, 0):
        start = block_start(rank, block, 4, hop)
        part = nt(mixed_out[pl.ds(start, block), :], back)
        if hop == 0:
            keep_own[...] = part
        elif hop == 2:
            keep_x[...] = part
        else:
            send[hop // 2] = part.astype(BF)


def memory_kernel(width, ids, ins, late, outs, saved, scratch):
    memory, seg, bias = ins[:3]
    parts = ins[3:]
    wide, pair = (item() for item in saved)
    place = ids[0]
    rows = memory[...]
    segments = seg[...]
    for group in range(2):
        place_padded(parts, place, wide.at[group], group)
    saved[0].flush()
    for group in range(2):
        pair[group, :, :LANES] = tag_keys(
            nn(rows, wide[group, :, LANES : 2 * LANES]), segments, width
        )
        pair[group, :, LANES:] = (
            nn(rows, wide[group, :, 2 * LANES : 3 * LANES]) + bias[group, 3:4, :]
        ).astype(BF)


def first_norm_kernel(ids, ins, late, outs, saved, scratch):
    keep, from_core, from_x, target, rowv = ins
    low_out, first_out = outs
    xhat_out, scale_out = (item() for item in saved)
    summed = keep[...] + from_core[0].astype(F32) + from_x[...].astype(F32) + rowv[0:1, :]
    xhat, scale = normalize(target[...].astype(F32) + summed)
    xhat_out[...] = xhat
    scale_out[...] = jnp.broadcast_to(scale, scale_out.shape)
    first = xhat * rowv[3:4, :] + rowv[4:5, :]
    first_out[...] = first
    low_out[...] = first.astype(BF)


def cross_kernel(width, ids, ins, late, outs, saved, scratch):
    own, core, seg, bias = ins
    wide, pair = late
    keep, send = outs
    state, lse_out = (item() for item in saved)
    block = own.shape[0]
    lse_out[...] = jnp.zeros_like(lse_out)
    for hop, low in ((1, core), (0, own)):
        at = slice(hop * block, (hop + 1) * block)
        segments = seg[at, :]
        branch = jnp.zeros((block, own.shape[1]), F32)
        for group in range(2):
            queries = tag_queries(
                (nn(low[...], wide()[group, :, :LANES]) + bias[group, 2:3, :]) * 0.125,
                segments,
                width,
            )
            state[group, at, :LANES] = queries

            def put_mixed(mixed):
                state[group, at, LANES:] = mixed

            def put_lse(head, row):
                lse_out[group, head : head + 1, at] = row

            attend(
                queries,
                pair()[group, :, :LANES],
                split_values(pair()[group, :, LANES:], width),
                width,
                None,
                put_mixed,
                put_lse,
            )
            branch = branch + nt(state[group, at, LANES:], wide()[group, :, 3 * LANES :])
        if hop:
            send[...] = branch.astype(BF)
        else:
            keep[...] = branch


def second_norm_kernel(ids, ins, late, outs, saved, scratch):
    keep, from_core, first, rowv = ins
    low_out, second_out = outs
    xhat_out, scale_out = (item() for item in saved)
    summed = first[...] + (keep[...] + from_core[...].astype(F32) + rowv[1:2, :])
    xhat, scale = normalize(summed)
    xhat_out[...] = xhat
    scale_out[...] = jnp.broadcast_to(scale, scale_out.shape)
    second = xhat * rowv[5:6, :] + rowv[6:7, :]
    second_out[...] = second
    low_out[...] = second.astype(BF)


def gelu_both(values):
    bell = jnp.exp(-0.5 * values * values)
    inverse = 1.0 / (1.0 + 0.23164189 * jnp.abs(values))
    tail = inverse * (
        0.127414796
        + inverse
        * (
            -0.142248368
            + inverse * (0.7107068705 + inverse * (-0.7265760135 + inverse * 0.5307027145))
        )
    )
    tail = tail * bell
    area = jnp.where(values < 0.0, tail, 1.0 - tail)
    return values * area, area + values * bell * 0.3989422804


def ffn_rows(rows, expand, contract, bias):
    hidden, slope = gelu_both(nn(rows, expand) + bias)
    hidden = hidden.astype(BF)
    return hidden, slope.astype(BF), nt(hidden, contract)


def ffn_kernel(ids, ins, late, outs, saved, scratch):
    own, core, bias = ins[:3]
    if len(outs) > 4:
        expand, contract, hidden_out, slope_out, keep, send = outs
        parts = ins[3:]
        place_plain(parts, ids[0], expand, 0)
        place_plain(parts, ids[0], contract, 1)
    else:
        expand, contract = ins[3:]
        hidden_out, slope_out, keep, send = outs
    block = own.shape[0]
    for hop, rows, out in ((1, core, send), (0, own, keep)):
        at = slice(hop * block, (hop + 1) * block)
        hidden, slope, part = ffn_rows(rows[...], expand[...], contract[...], bias[...])
        hidden_out[at, :] = hidden
        slope_out[at, :] = slope
        out[...] = part.astype(out.dtype)


def last_norm_kernel(ids, ins, late, outs, saved, scratch):
    keep, from_core, from_x, second, cotangent, rowv = ins
    output, low_out, grad_out, sums = outs
    summed = keep[...] + from_core[...].astype(F32) + from_x[...].astype(F32) + rowv[2:3, :]
    xhat, scale = normalize(second[...] + summed)
    output[...] = (xhat * rowv[7:8, :] + rowv[8:9, :]).astype(BF)
    grad = cotangent[...].astype(F32)
    back = norm_back(grad, xhat, scale, rowv[7:8, :])
    grad_out[...] = back
    low = back.astype(BF)
    low_out[...] = low
    put_sums(sums, low, grad, xhat)


def put_sums(sums, low, grad, normed):
    sums[...] = jnp.zeros_like(sums)
    sums[0:1, :] = col_sum(low.astype(F32))
    sums[1:2, :] = col_sum(grad * normed)
    sums[2:3, :] = col_sum(grad)


def ffn_back_kernel(ids, ins, late, outs, saved, scratch):
    own, core, expand, contract, slope = ins
    pre_out, keep, send = outs
    block = own.shape[0]
    for hop, rows, out in ((1, core, send), (0, own, keep)):
        at = slice(hop * block, (hop + 1) * block)
        grad = (slope[at, :].astype(F32) * nn(rows[...], contract[...])).astype(BF)
        pre_out[at, :] = grad
        out[...] = nt(grad, expand[...]).astype(out.dtype)


def put_blocks(total, place, outs, hops, pack=None):
    if len(outs[0].shape) < 4 - len(outs[1:]):
        if pack is None:
            outs[0][...] = total[...].astype(BF)
        else:
            outs[0][pack] = total[...].astype(BF)
        return
    rows = outs[0].shape[-2]
    level = jnp.right_shift(place, 1)
    for step in range(4):
        for side in range(2):
            index = 2 * (jnp.bitwise_xor(level, step) if hops else step)
            if len(outs) == 2:
                index = index + jnp.bitwise_xor(jnp.bitwise_and(place, 1), side)
                out = outs[side].at[step]
            else:
                index = index + side
                out = outs[0].at[side, step]
            if not isinstance(index, int):
                index = pl.multiple_of(index * rows, rows)
            else:
                index = index * rows
            value = total[pl.ds(index, rows), :].astype(BF)
            if pack is None:
                out[...] = value
            else:
                out[pack] = value


def ffn_grad_kernel(ids, ins, late, outs, saved, scratch):
    rows, grads = ins[:4], ins[4:8]
    hidden_near, hidden_far, pre_near, pre_far = ins[8:]
    (total,) = scratch
    sums, keep = outs
    place = ids[0]
    block = rows[0].shape[0]

    def half(ref, hop):
        return ref[(hop % 2) * block : (hop % 2 + 1) * block, :]

    sums[...] = jnp.zeros_like(sums)
    sums[0:1, :] = col_sum(pre_near[...].astype(F32)) + col_sum(pre_far[...].astype(F32))
    for which, left, near, far in ((1, grads, hidden_near, hidden_far), (0, rows, pre_near, pre_far)):
        for hop in range(4):
            part = tn(left[hop][...], half(far if hop // 2 else near, hop))
            if hop == 0:
                total[...] = part
            else:
                total[...] += part
        put_blocks(total, place, [keep], False, which)


def second_back_kernel(ids, ins, late, outs, saved, scratch):
    keep, from_core, from_x, grad3, rowv = ins
    xhat, scale = late
    low_out, grad_out, sums = outs
    grad = grad3[...] + keep[...] + from_core[...].astype(F32) + from_x[...].astype(F32)
    normed = xhat()[...]
    grad2 = norm_back(grad, normed, scale()[:, 0:1], rowv[5:6, :])
    grad_out[...] = grad2
    low = grad2.astype(BF)
    low_out[...] = low
    put_sums(sums, low, grad, normed)


def first_back_kernel(ids, ins, late, outs, saved, scratch):
    keep, from_core, grad2, rowv = ins
    xhat, scale = late
    low_out, grad_out, sums = outs
    grad = grad2[...] + keep[...] + from_core[...].astype(F32)
    normed = xhat()[...]
    grad1 = norm_back(grad, normed, scale()[:, 0:1], rowv[3:4, :])
    grad_out[...] = grad1
    low = grad1.astype(BF)
    low_out[...] = low
    put_sums(sums, low, grad, normed)


def cross_back_kernel(width, ids, ins, late, outs, saved, scratch):
    own, core = ins
    wide, pair, state, lse = late
    dq_out, dk_out, dv_out, keep, send, bias_sums = outs
    dk_acc, dv_acc = scratch
    block = own.shape[0]
    bias_sums[...] = jnp.zeros_like(bias_sums)
    dk_acc[...] = jnp.zeros_like(dk_acc)
    dv_acc[...] = jnp.zeros_like(dv_acc)
    keys_t = None
    for hop, low in ((1, core), (0, own)):
        at = slice(hop * block, (hop + 1) * block)
        total = jnp.zeros((block, own.shape[1]), F32)
        if keys_t is None:
            keys_t = [transposed(pair()[group, :, :LANES]) for group in range(2)]
        for group in range(2):
            grad_mixed = nn(low[...], wide()[group, :, 3 * LANES :]).astype(BF)

            def add_key(value):
                dk_acc[group] += value

            def add_value(value):
                dv_acc[group] += value

            dq = attend_back(
                state()[group, at, :LANES],
                pair()[group, :, :LANES],
                pair()[group, :, LANES:],
                keys_t[group],
                grad_mixed,
                state()[group, at, LANES:],
                lambda head: lse()[group, head : head + 1, at],
                width,
                None,
                add_key,
                add_value,
            )
            dq_low = (dq.astype(BF).astype(F32) * 0.125).astype(BF)
            dq_out[group, at, :] = dq_low
            bias_sums[group, 0:1, :] += col_sum(dq_low.astype(F32))
            total = total + nt(dq_low, wide()[group, :, :LANES])
        if hop:
            send[...] = total.astype(BF)
        else:
            keep[...] = total
    for group in range(2):
        dk_out[group] = dk_acc[group].astype(BF)
        dv_low = dv_acc[group].astype(BF)
        dv_out[group] = dv_low
        bias_sums[group, 1:2, :] = col_sum(dv_low.astype(F32))


def cross_grad_kernel(width, ids, ins, late, outs, saved, scratch):
    dq, dk, dv, low_two, low_two_core, low1, low1_core = ins
    wide, state, memory = late
    (total,) = scratch
    mem_keep, mem_x, mem_send = outs[:3]
    place, rank = ids[0], ids[1]
    block = mem_keep.shape[0]
    rows = low1.shape[0]
    for group in range(2):
        total[:, 3 * width :] = (
            tn(low_two[...], state()[group, :rows, LANES:])
            + tn(low_two_core[...], state()[group, rows:, LANES:])
        )[:, :width]
        total[:, :width] = (
            tn(low1[...], dq[group, :rows, :]) + tn(low1_core[...], dq[group, rows:, :])
        )[:, :width]
        total[:, width : 2 * width] = tn(memory()[...], dk[group])[:, :width]
        total[:, 2 * width : 3 * width] = tn(memory()[...], dv[group])[:, :width]
        put_blocks(total, place, outs[3:], True, group)
    for hop in (1, 3, 2, 0):
        start = block_start(rank, block, 4, hop)
        part = jnp.zeros((block, wide().shape[1]), F32)
        for group in range(2):
            part = part + nt(dk[group, pl.ds(start, block), :], wide()[group, :, LANES : 2 * LANES])
            part = part + nt(
                dv[group, pl.ds(start, block), :], wide()[group, :, 2 * LANES : 3 * LANES]
            )
        if hop == 0:
            mem_keep[...] = part
        elif hop == 2:
            mem_x[...] = part
        else:
            mem_send[hop // 2] = part.astype(BF)


def self_back_kernel(width, ids, ins, late, outs, saved, scratch):
    grads = ins
    wide, state, lse, target = late
    low, total, dk_acc, dv_acc = scratch
    three, bias_sums, keep = outs
    place, rank = ids[0], ids[1]
    length = low.shape[0]
    block = length // 4
    place_plain(grads, rank, low)
    grad_mixed = nn(low[...], wide()[:, 3 * LANES :]).astype(BF)
    q_in, k_in, v_in, mixed = (state().at[:, i * LANES : (i + 1) * LANES] for i in range(4))
    keys_t = transposed(k_in[...])
    dk_acc[...] = jnp.zeros_like(dk_acc)
    dv_acc[...] = jnp.zeros_like(dv_acc)
    bias_sums[...] = jnp.zeros_like(bias_sums)
    for index in range(4):
        start, stop = index * block, (index + 1) * block

        def add_key(value):
            dk_acc[:stop, :] += value

        def add_value(value):
            dv_acc[:stop, :] += value

        dq = attend_back(
            q_in[start:stop, :],
            k_in[:stop, :],
            v_in[:stop, :],
            keys_t[:, :stop],
            grad_mixed[start:stop],
            mixed[start:stop, :],
            lambda head: lse()[head : head + 1, start:stop],
            width,
            start,
            add_key,
            add_value,
        )
        three[start:stop, :LANES] = (dq.astype(BF).astype(F32) * 0.125).astype(BF)
    three[:, LANES : 2 * LANES] = dk_acc[...].astype(BF)
    three[:, 2 * LANES :] = dv_acc[...].astype(BF)
    bias_sums[0:1, :] = col_sum(three[:, :LANES].astype(F32))
    bias_sums[1:2, :] = col_sum(three[:, 2 * LANES :].astype(F32))
    part = tn(target()[...], three[...])
    for group in range(3):
        total[:, group * width : (group + 1) * width] = part[
            :, group * LANES : group * LANES + width
        ]
    total[:, 3 * width :] = tn(low[...], mixed[...])[:, :width]
    put_blocks(total, place, [keep], True)


def target_kernel(ids, ins, late, outs, saved, scratch):
    (three,) = ins
    (wide,) = late
    keep, keep_x, send = outs
    rank = ids[1]
    block = keep.shape[0]
    for hop in (3, 1, 2, 0):
        start = block_start(rank, block, 4, hop)
        part = nt(three[pl.ds(start, block), :], wide()[:, : 3 * LANES])
        if hop == 0:
            keep[...] = part
        elif hop == 2:
            keep_x[...] = part
        else:
            send[hop // 2] = part.astype(BF)


def join_kernel(ids, ins, late, outs, saved, scratch):
    rank = ids[1]
    block = ins[0].shape[0]
    for hop, part in enumerate(ins):
        outs[0][pl.ds(block_start(rank, block, 4, hop), block), :] = part[...].astype(outs[0].dtype)


def adam(weight, gradient, moment, square, rate, clip_scale):
    clipped = gradient * clip_scale
    new_moment = BETA_ONE * moment + (1.0 - BETA_ONE) * clipped
    new_square = BETA_TWO * square + (1.0 - BETA_TWO) * clipped * clipped
    fixed_moment = new_moment / (1.0 - BETA_ONE**STEP)
    fixed_square = new_square / (1.0 - BETA_TWO**STEP)
    new_weight = weight - rate * (
        fixed_moment / (jnp.sqrt(fixed_square) + ADAM_EPS) + DECAY * weight
    )
    return (new_weight, new_moment, new_square)


def local(
    data_size,
    tensor_size,
    target,
    memory,
    target_segments,
    memory_segments,
    cotangent,
    input_weights,
    input_moment,
    input_square,
    output_weights,
    output_moment,
    output_square,
    expand_weights,
    expand_moment,
    expand_square,
    contract_weights,
    contract_moment,
    contract_square,
    head_biases,
    head_moment,
    head_square,
    hidden_biases,
    hidden_moment,
    hidden_square,
    row_vectors,
    row_moment,
    row_square,
):
    length, model = target.shape[1:]
    mem_length = memory.shape[1]
    width = head_biases.shape[1]
    block = length // tensor_size
    mem_block = mem_length // tensor_size
    share = model // data_size
    direct = data_size == 8 and share % 16 == 0
    place = lax.axis_index("dp")
    rank = lax.axis_index("tensor")
    ids = jnp.stack([place, rank]).astype(jnp.int32)
    target_rows = target.reshape(length, model)
    memory_rows = memory.reshape(mem_length, model)
    cotangent_rows = cotangent.reshape(length, model)
    target_seg = target_segments.reshape(length, 1)
    memory_seg = memory_segments.reshape(mem_length, 1)
    rowv = jnp.pad(row_vectors, ((0, 7), (0, 0)))
    bias = jnp.pad(head_biases, ((0, 4), (0, LANES - width)))

    def to_tensor(value, hop):
        return lax.ppermute(value, "tensor", [(i, i ^ hop) for i in range(tensor_size)])

    def to_data(value, hop):
        return lax.ppermute(value, "dp", [(i, i ^ hop) for i in range(data_size)])

    def over_z(value):
        groups = [list(range(side, data_size, 2)) for side in range(2)]
        return lax.all_to_all(value, "dp", 0, 0, axis_index_groups=groups, tiled=True)

    def gather_plain(value):
        return [lax.all_gather(value, "dp", axis=value.ndim - 2, tiled=True)]

    def spread(value):
        return over_z(jnp.broadcast_to(value[None], (4,) + value.shape))

    def over_y(value):
        groups = [[side, side + 1] for side in range(0, data_size, 2)]
        return lax.all_to_all(value, "dp", 0, 0, axis_index_groups=groups, tiled=True)

    def added(received):
        return (received[0].astype(F32) + received[1].astype(F32)).astype(BF)

    def hops_z(value):
        return [value[0]] + [to_data(value[hop], 2 * hop) for hop in (1, 2, 3)]

    def total_of(received):
        first, second, third, fourth = (part.astype(F32) for part in received)
        return (first + second) + (third + fourth)

    def scatter_plain(value):
        return lax.psum_scatter(
            value, "dp", scatter_dimension=value.ndim - 2, tiled=True
        ).astype(F32)

    def sum_data(value):
        if not direct:
            return lax.psum(value, "dp")
        value = value + to_data(value, 1)
        got = [to_data(value, hop) for hop in (2, 4, 6)]
        return (value + got[0]) + (got[1] + got[2])

    def join(own, far, dtype):
        core = to_tensor(own, 1)
        diag = to_tensor(far, 1)
        rows = own.shape[0] * 4
        return call(
            join_kernel, ids, [own, core, far, diag], [], [SDS((rows, model), dtype)], [], name="join"
        )[0]

    def sum_rows(keep_x, send_x):
        return (keep_x + send_x.astype(F32)).astype(BF)

    self_pack = jnp.concatenate(
        [input_weights[0], input_weights[1], input_weights[2], output_weights[0].T], axis=1
    ).astype(BF)
    cross_pack = jnp.concatenate(
        [input_weights[3], input_weights[4], input_weights[5], output_weights[1].T], axis=1
    ).astype(BF)
    cross_far = to_tensor(cross_pack, 2)
    bias_far = to_tensor(bias, 2)
    target_own = lax.dynamic_slice_in_dim(target_rows, rank * block, block, 0)
    cotangent_own = lax.dynamic_slice_in_dim(cotangent_rows, rank * block, block, 0)
    seg_near = jnp.concatenate(
        [
            lax.dynamic_slice_in_dim(target_seg, (rank ^ hop) * block, block, 0)
            for hop in range(2)
        ]
    )
    cross_pair = jnp.stack([cross_pack, cross_far])
    ffn_pair = jnp.stack([expand_weights.astype(BF), contract_weights.T.astype(BF)])
    if direct:
        self_z = [to_data(self_pack, hop) for hop in (2, 4, 6)]
        self_parts = [self_pack, to_data(self_pack, 1)]
        for part in self_z:
            self_parts += [part, to_data(part, 1)]
        cross_parts = [spread(after(cross_pair, *self_z, self_parts[3], self_parts[5]))]
        cross_parts.append(to_data(cross_parts[0], 1))
    else:
        self_parts, cross_parts = gather_plain(self_pack), gather_plain(cross_pair)
    cross_bias = jnp.stack([bias, bias_far])

    quarter = SDS((block, model), F32)
    quarter_low = SDS((block, model), BF)
    pair_low = SDS((2, block, model), BF)
    column = SDS((block, 128), F32)
    sums_shape = SDS((8, model), F32)
    padded = 4 * LANES

    (keep, keep_x, send, wide_self, state_self, lse_self) = call(
        partial(self_kernel, width),
        ids,
        [target_rows, target_seg, bias, *self_parts],
        [],
        [quarter, quarter, pair_low],
        [SDS((model, padded), BF), SDS((length, padded), BF), SDS((8, length), F32)],
        flops=2 * length * model * padded + 8 * length * length * LANES,
        name="self_forward",
    )
    from_core = to_tensor(send, 1)
    to_far = sum_rows(keep_x, from_core[1])
    from_x = to_tensor(to_far, 2)
    if direct:
        ffn_parts = [spread(after(ffn_pair, to_far))]
        ffn_parts.append(to_data(ffn_parts[0], 1))
    else:
        ffn_parts = gather_plain(ffn_pair)

    mem_rows = SDS((2, mem_length, LANES), BF)
    wide_cross, kv_cross = call(
        partial(memory_kernel, width),
        ids,
        [memory_rows, memory_seg, cross_bias, *cross_parts],
        [],
        [],
        [SDS((2, model, padded), BF), SDS((2, mem_length, 2 * LANES), BF)],
        flops=8 * mem_length * model * LANES,
        name="memory_rows",
    )
    low1, first, xhat1, scale1 = call(
        first_norm_kernel,
        ids,
        [keep, from_core, from_x, target_own, rowv],
        [],
        [quarter_low, quarter],
        [quarter, column],
        name="first_norm",
    )
    low1_core = to_tensor(low1, 1)
    pair_rows = SDS((2, 2 * block, LANES), BF)
    keep, send, state_cross, lse_cross = call(
        partial(cross_kernel, width),
        ids,
        [low1, low1_core, seg_near, cross_bias],
        [wide_cross, kv_cross],
        [quarter, quarter_low],
        [SDS((2, 2 * block, 2 * LANES), BF), SDS((2, 8, 2 * block), F32)],
        flops=16 * block * model * LANES + 48 * block * mem_length * LANES,
        name="cross_forward",
    )
    low2, second, xhat2, scale2 = call(
        second_norm_kernel,
        ids,
        [keep, to_tensor(send, 1), first, rowv],
        [],
        [quarter_low, quarter],
        [quarter, column],
        name="second_norm",
    )

    low2_x = to_tensor(low2, 2)
    low2_core = to_tensor(low2, 1)
    hidden_row = hidden_biases.reshape(1, -1)
    units = hidden_row.shape[1]
    half_units = SDS((2 * block, units), BF)
    ffn_flops = 8 * block * model * units
    expand_all, contract_all, hidden_near, slope_near, keep, send = call(
        ffn_kernel,
        ids,
        [low2, low2_core, hidden_row, *ffn_parts],
        [],
        [SDS((model, units), BF)] * 2 + [half_units, half_units, quarter, quarter_low],
        [],
        flops=ffn_flops,
        name="ffn_near",
    )
    from_core = to_tensor(send, 1)
    low2_diag = to_tensor(low2_x, 1)
    hidden_far, slope_far, keep_x, send = call(
        ffn_kernel,
        ids,
        [low2_x, low2_diag, hidden_row, expand_all, contract_all],
        [],
        [half_units, half_units, quarter, quarter_low],
        [],
        flops=ffn_flops,
        name="ffn_far",
    )
    from_x = to_tensor(sum_rows(keep_x, to_tensor(send, 1)), 2)
    out_own, low3, grad3, sums3 = call(
        last_norm_kernel,
        ids,
        [keep, from_core, from_x, second, cotangent_own, rowv],
        [],
        [quarter_low, quarter_low, quarter, sums_shape],
        [],
        name="last_norm",
    )

    low3_x = to_tensor(low3, 2)
    low3_core = to_tensor(low3, 1)
    pre_near, keep, send = call(
        ffn_back_kernel,
        ids,
        [low3, low3_core, expand_all, contract_all, slope_near],
        [],
        [half_units, quarter, quarter_low],
        [],
        flops=ffn_flops,
        name="ffn_back_near",
    )
    from_core = to_tensor(send, 1)
    low3_diag = to_tensor(low3_x, 1)
    pre_far, keep_x, send = call(
        ffn_back_kernel,
        ids,
        [low3_x, low3_diag, expand_all, contract_all, slope_far],
        [],
        [half_units, quarter, quarter_low],
        [],
        flops=ffn_flops,
        name="ffn_back_far",
    )
    to_far = sum_rows(keep_x, to_tensor(send, 1))
    from_x = to_tensor(to_far, 2)
    blocks = SDS((2, 4, share, model), BF) if direct else SDS((model, model), BF)
    pair = SDS((2, 4, 2, share, model), BF) if direct else SDS((2, model, model), BF)
    ffn_outs = call(
        ffn_grad_kernel,
        ids,
        [after(low2, to_far), low2_core, low2_x, low2_diag, low3, low3_core, low3_x, low3_diag]
        + [hidden_near, hidden_far, pre_near, pre_far],
        [],
        [SDS((8, units), F32)] + [pair],
        [],
        [pltpu.VMEM((model, units), F32)],
        flops=2 * ffn_flops,
        name="ffn_grad",
    )
    hidden_sums = ffn_outs[0]
    ffn_along = over_y(ffn_outs[1]) if direct else None

    low_two, grad2, sums2 = call(
        second_back_kernel,
        ids,
        [after(keep, ffn_outs[1]), from_core, from_x, grad3, rowv],
        [xhat2, scale2],
        [quarter_low, quarter, sums_shape],
        [],
        name="second_back",
    )
    low_two_core = to_tensor(low_two, 1)
    output_far = to_tensor(after(out_own, low_two), 2)
    dq, dk, dv, keep, send, bias_sums = call(
        partial(cross_back_kernel, width),
        ids,
        [low_two, low_two_core],
        [wide_cross, kv_cross, state_cross, lse_cross],
        [pair_rows, mem_rows, mem_rows, quarter, quarter_low, SDS((2, 8, LANES), F32)],
        [],
        [pltpu.VMEM((2, mem_length, LANES), F32)] * 2,
        flops=16 * block * model * LANES + 120 * block * mem_length * LANES,
        name="cross_back",
    )
    mem_quarter = SDS((mem_block, model), F32)
    cross_outs = call(
        partial(cross_grad_kernel, width),
        ids,
        [dq, dk, dv, low_two, low_two_core, low1, low1_core],
        [wide_cross, state_cross, memory_rows],
        [mem_quarter, mem_quarter, SDS((2, mem_block, model), BF)]
        + ([SDS((4, 2, share, model), BF)] * 2 if direct else [pair]),
        [],
        [pltpu.VMEM((model, model), F32)],
        flops=24 * mem_length * model * LANES,
        name="cross_grad",
    )
    mem_keep, mem_x, mem_send = cross_outs[:3]
    cross_along = to_data(cross_outs[4], 1) if direct else None

    low_one, grad1, sums1 = call(
        first_back_kernel,
        ids,
        [after(keep, cross_outs[0]), to_tensor(after(send, output_far), 1), grad2, rowv],
        [xhat1, scale1],
        [quarter_low, quarter, sums_shape],
        [],
        name="first_back",
    )
    low_one_x = to_tensor(low_one, 2)
    low_one_core = to_tensor(low_one, 1)
    if direct:
        ffn_received = over_z(added(after(ffn_along, low_one_core)))
    low_one_diag = to_tensor(low_one_x, 1)

    back_outs = call(
        partial(self_back_kernel, width),
        ids,
        [low_one, low_one_core, low_one_x, low_one_diag],
        [wide_self, state_self, lse_self, target_rows],
        [SDS((length, 3 * LANES), BF), SDS((8, LANES), F32)] + [blocks],
        [],
        [pltpu.VMEM((length, model), BF), pltpu.VMEM((model, model), F32)]
        + [pltpu.VMEM((length, LANES), F32)] * 2,
        flops=4 * length * model * padded + 20 * length * length * LANES,
        name="self_back",
    )
    three, self_sums, keep_self = back_outs[:3]
    if direct:
        self_along = over_y(keep_self)
        late_rows = after(jnp.stack(
            [sums1[0], sums2[0], sums3[0], sums1[1], sums1[2], sums2[1], sums2[2], sums3[1], sums3[2]]
        ), self_along)
        cross_received = hops_z(added((cross_outs[3], cross_along)))
        self_received = hops_z(added(self_along))
        ffn_share = total_of(ffn_received)
        cross_both = total_of(cross_received)
        self_share = total_of(self_received)
    else:
        ffn_share = scatter_plain(ffn_outs[1])
        cross_both = scatter_plain(cross_outs[3])
        self_share = scatter_plain(keep_self)
        late_rows = jnp.stack(
            [sums1[0], sums2[0], sums3[0], sums1[1], sums1[2], sums2[1], sums2[2], sums3[1], sums3[2]]
        )
    cross_share = cross_both[0] + to_tensor(cross_both[1].astype(BF), 2).astype(F32)
    expand_share, contract_share = ffn_share[0], ffn_share[1]

    keep, keep_x, send = call(
        target_kernel,
        ids,
        [three],
        [wide_self],
        [quarter, quarter, pair_low],
        [],
        flops=6 * length * model * LANES,
        name="target_grad",
    )
    from_core = to_tensor(send, 1)
    from_x = to_tensor(sum_rows(keep_x, from_core[1]), 2)
    target_sum = (grad1 + keep + from_core[0].astype(F32) + from_x.astype(F32)).astype(BF)
    from_core = to_tensor(after(mem_send, three), 1)
    from_x = to_tensor(sum_rows(mem_x, from_core[1]), 2)
    memory_sum = (mem_keep + from_core[0].astype(F32) + from_x.astype(F32)).astype(BF)

    output = join(out_own, output_far, BF)
    memory_far = to_tensor(memory_sum, 2)
    memory_grad = join(memory_sum, memory_far, F32)
    target_far = to_tensor(target_sum, 2)
    target_grad = join(target_sum, target_far, F32)

    row_part = late_rows
    row_part = row_part + to_tensor(row_part, 1)
    row_part = row_part + to_tensor(row_part, 2)
    cross_sums = bias_sums[:, :2, :width]
    near = cross_sums[0] + to_tensor(cross_sums[1], 2)
    head_part = jnp.concatenate([self_sums[:2, :width], near], axis=0)
    small = sum_data(
        jnp.concatenate([row_part, head_part.reshape(1, -1), hidden_sums[:1]], axis=0)
    )
    row_grad = small[:9]
    head_grad = small[9].reshape(4, width)
    hidden_grad = small[10]

    own_squares = (
        jnp.sum(self_share * self_share)
        + jnp.sum(cross_share * cross_share)
        + jnp.sum(expand_share * expand_share)
        + jnp.sum(contract_share * contract_share)
    )
    shared_squares = (
        jnp.sum(head_grad * head_grad) + jnp.sum(hidden_grad * hidden_grad)
    ) / data_size
    common_squares = jnp.sum(row_grad * row_grad) / (data_size * tensor_size)
    squares = (own_squares + shared_squares + common_squares).reshape(1, 1)
    squares = after(squares, target_far, memory_far)
    squares = squares + to_tensor(squares, 1)
    squares = squares + to_tensor(squares, 2)
    grad_norm = jnp.sqrt(sum_data(squares)[0, 0])
    clip_scale = jnp.minimum(1.0, MAX_NORM / (grad_norm + 1e-06))

    input_share = jnp.stack(
        [pack[:, i * width : (i + 1) * width] for pack in (self_share, cross_share) for i in range(3)]
    )
    output_share = jnp.stack([self_share[:, 3 * width :].T, cross_share[:, 3 * width :].T])
    in_new = adam(input_weights, input_share, input_moment, input_square, RATE_MATRIX, clip_scale)
    out_new = adam(
        output_weights, output_share, output_moment, output_square, RATE_MATRIX, clip_scale
    )
    expand_new = adam(
        expand_weights, expand_share, expand_moment, expand_square, RATE_MATRIX, clip_scale
    )
    contract_new = adam(
        contract_weights, contract_share.T, contract_moment, contract_square, RATE_MATRIX, clip_scale
    )
    head_new = adam(head_biases, head_grad, head_moment, head_square, RATE_VECTOR, clip_scale)
    hidden_new = adam(
        hidden_biases, hidden_grad, hidden_moment, hidden_square, RATE_VECTOR, clip_scale
    )
    row_new = adam(row_vectors, row_grad, row_moment, row_square, RATE_VECTOR, clip_scale)
    return (
        output.reshape(target.shape),
        target_grad.reshape(target.shape),
        memory_grad.reshape(memory.shape),
        grad_norm,
        in_new[0],
        in_new[1],
        in_new[2],
        in_new[0].astype(BF),
        out_new[0],
        out_new[1],
        out_new[2],
        out_new[0].astype(BF),
        expand_new[0],
        expand_new[1],
        expand_new[2],
        expand_new[0].astype(BF),
        contract_new[0],
        contract_new[1],
        contract_new[2],
        contract_new[0].astype(BF),
        head_new[0],
        head_new[1],
        head_new[2],
        hidden_new[0],
        hidden_new[1],
        hidden_new[2],
        row_new[0],
        row_new[1],
        row_new[2],
    )


def solution(mesh):
    rows = P("dp", None, None)
    in_matrix = P(None, "dp", "tensor")
    out_matrix = P(None, "tensor", "dp")
    return jax.shard_map(
        partial(local, mesh.shape["dp"], mesh.shape["tensor"]),
        mesh=mesh,
        in_specs=(rows, rows, P("dp", None), P("dp", None), rows)
        + (in_matrix,) * 3
        + (out_matrix,) * 3
        + (P("dp", "tensor"),) * 3
        + (P("tensor", "dp"),) * 3
        + (P(None, "tensor"),) * 3
        + (P("tensor"),) * 3
        + (P(),) * 3,
        out_specs=(rows, rows, rows, P())
        + (in_matrix,) * 4
        + (out_matrix,) * 4
        + (P("dp", "tensor"),) * 4
        + (P("tensor", "dp"),) * 4
        + (P(None, "tensor"),) * 3
        + (P("tensor"),) * 3
        + (P(),) * 3,
        check_vma=False,
    )
```

```python
from functools import partial

import jax
import jax.numpy as jnp
from jax import lax
from jax.experimental import pallas as pl
from jax.experimental.pallas import tpu as pltpu
from jax.sharding import PartitionSpec as P

HEAD_DIM = 64
STEP = 10
NORM_EPS = 1e-05
BETA_ONE = 0.9
BETA_TWO = 0.999
RATE_MATRIX = 0.06
RATE_VECTOR = 0.5
DECAY = 0.01
ADAM_EPS = 1e-08
MAX_NORM = 1.0
BIG = 1e30
LANES = 256
MIB = 2**20
COST = 1.0

BF = jnp.bfloat16
F32 = jnp.float32
SDS = jax.ShapeDtypeStruct


def nn(left, right):
    return jnp.dot(left, right, preferred_element_type=F32)


def nt(left, right):
    return lax.dot_general(left, right, (((1,), (1,)), ((), ())), preferred_element_type=F32)


def tn(left, right):
    return lax.dot_general(left, right, (((0,), (0,)), ((), ())), preferred_element_type=F32)


def iota(shape, dim):
    return lax.broadcasted_iota(jnp.int32, shape, dim)


class Late:
    def __init__(self, copy, buffer):
        self.copy, self.buffer, self.waited = copy, buffer, False

    def __call__(self):
        if not self.waited:
            self.copy.wait()
            self.waited = True
        return self.buffer


class Saved:
    def __init__(self, copy, buffer):
        self.copy, self.buffer, self.started = copy, buffer, False

    def __call__(self):
        return self.buffer

    def flush(self):
        self.copy.start()
        self.started = True


def call(body, ids, ins, late, outs, saved, scratch=(), flops=0, vmem=32, name=None):
    counts = [len(ins), len(late), len(outs), len(saved), len(late), len(saved), len(scratch)]

    def kernel(ids_ref, *refs):
        groups = []
        start = 0
        for number in counts:
            groups.append(refs[start : start + number])
            start += number
        in_refs, late_refs, out_refs, saved_refs, late_bufs, saved_bufs, extra = groups
        sems = refs[start] if late or saved else None
        lates = [
            Late(pltpu.make_async_copy(ref, buf, sems.at[i]), buf)
            for i, (ref, buf) in enumerate(zip(late_refs, late_bufs))
        ]
        for item in lates:
            item.copy.start()
        saves = [
            Saved(pltpu.make_async_copy(buf, ref, sems.at[len(late) + i]), buf)
            for i, (ref, buf) in enumerate(zip(saved_refs, saved_bufs))
        ]
        body(ids_ref, in_refs, lates, out_refs, saves, extra)
        for item in lates:
            item()
        for item in saves:
            if not item.started:
                item.flush()
        for item in saves:
            item.copy.wait()

    size = sum(a.size * a.dtype.itemsize for a in [*ins, *late])
    size += sum(o.size * o.dtype.itemsize for o in [*outs, *saved])
    vmem_spec = pl.BlockSpec(memory_space=pltpu.VMEM)
    hbm_spec = pl.BlockSpec(memory_space=pltpu.HBM)
    sems = [pltpu.SemaphoreType.DMA((len(late) + len(saved),))] if late or saved else []
    result = pl.pallas_call(
        kernel,
        out_shape=[*outs, *saved],
        in_specs=[pl.BlockSpec(memory_space=pltpu.SMEM)]
        + [vmem_spec] * len(ins)
        + [hbm_spec] * len(late),
        out_specs=[vmem_spec] * len(outs) + [hbm_spec] * len(saved),
        scratch_shapes=[pltpu.VMEM(a.shape, a.dtype) for a in [*late, *saved]]
        + list(scratch)
        + sems,
        compiler_params=pltpu.CompilerParams(vmem_limit_bytes=vmem * MIB),
        cost_estimate=pl.CostEstimate(
            flops=int(flops * COST), bytes_accessed=int(size * COST), transcendentals=0
        ),
        name=name,
    )(ids, *ins, *late)
    return result


def after(value, *others):
    if not others:
        return value
    return lax.optimization_barrier((value, *others))[0]


def block_start(index, rows, blocks, hop):
    if blocks == 1:
        return 0
    return pl.multiple_of(jnp.bitwise_xor(index, hop) * rows, rows)


def pieces(parts, place, pack):
    if len(parts) == 2:
        side = jnp.bitwise_and(place, 1)
        rows = parts[0].shape[2]
        for half, part in enumerate(parts):
            for level in range(4):
                index = 2 * level + jnp.bitwise_xor(side, half)
                yield part.at[level, pack], pl.multiple_of(index * rows, rows)
    else:
        for hop, part in enumerate(parts):
            block = part if pack is None else part.at[pack]
            rows = block.shape[0]
            yield block, block_start(place, rows, len(parts), hop)


def place_padded(parts, place, out, pack=None):
    width = parts[0].shape[-1] // 4
    for group in range(4):
        out[:, group * LANES + width : (group + 1) * LANES] = jnp.zeros(
            (out.shape[0], LANES - width), BF
        )
    for part, start in pieces(parts, place, pack):
        for group in range(4):
            out[pl.ds(start, part.shape[0]), group * LANES : group * LANES + width] = part[
                :, group * width : (group + 1) * width
            ]


def place_plain(parts, place, out, pack=None):
    for part, start in pieces(parts, place, pack):
        out[pl.ds(start, part.shape[0]), :] = part[...]


def normalize(values):
    center = jnp.mean(values, axis=-1, keepdims=True)
    centered = values - center
    spread = jnp.mean(centered * centered, axis=-1, keepdims=True)
    scale_row = lax.rsqrt(spread + NORM_EPS)
    return centered * scale_row, scale_row


def norm_back(grad_out, normed, scale_row, gain):
    scaled = grad_out * gain
    return scale_row * (
        scaled
        - jnp.mean(scaled, axis=-1, keepdims=True)
        - normed * jnp.mean(scaled * normed, axis=-1, keepdims=True)
    )


def col_sum(values):
    return jnp.sum(values, axis=0, keepdims=True)


def head_mask(rows, width, head):
    lane = iota((rows, LANES), 1)
    return (lane >= head * HEAD_DIM) & (lane < (head + 1) * HEAD_DIM)


def tag_queries(queries, seg, width):
    doc = iota(queries.shape, 1) - width
    tagged = (doc >= 0) & (doc < 4)
    return jnp.where(tagged, jnp.where(doc == seg, 0.0, -BIG), queries).astype(BF)


def tag_keys(keys, seg, width):
    doc = iota(keys.shape, 1) - width
    return jnp.where(doc == seg, 1.0, keys).astype(BF)


def attend(queries, keys, values, width, causal_from, mixed_out, logsum_out):
    rows = queries.shape[0]
    count = keys.shape[0]
    lane = iota((rows, LANES), 1)
    mixed = jnp.zeros((rows, LANES), F32)
    for head in range(width // HEAD_DIM):
        mask = head_mask(rows, width, head) | (lane >= width)
        scores = nt(jnp.where(mask, queries, jnp.zeros_like(queries)), keys)
        if causal_from is not None:
            ahead = iota((rows, rows), 1) <= iota((rows, rows), 0)
            last = jnp.where(ahead, scores[:, causal_from:], -BIG)
            if causal_from:
                scores = jnp.concatenate([scores[:, :causal_from], last], 1)
            else:
                scores = last
        top = jnp.max(scores, axis=1, keepdims=True)
        weights = jnp.exp(scores - top)
        total = jnp.sum(weights, axis=1, keepdims=True)
        mixed = mixed + nn(weights.astype(BF), values[head]) * (1.0 / total)
        logsum_out(head, (top + jnp.log(total)).reshape(1, rows))
    mixed_out(mixed.astype(BF))


def attend_back(queries, keys, values, keys_t, grad, mixed, logsum, width, causal_from, add_key, add_value):
    rows = queries.shape[0]
    lane = iota((rows, LANES), 1)
    along = (grad.astype(F32) * mixed.astype(F32)).T
    parts = []
    zero = jnp.zeros_like(queries)
    for head in range(width // HEAD_DIM):
        low, high = head * HEAD_DIM, (head + 1) * HEAD_DIM
        mask = head_mask(rows, width, head)
        own_query = jnp.where(mask, queries, zero)
        own_grad = jnp.where(mask, grad, zero)
        scores = nt(keys, jnp.where(lane >= width, queries, own_query))
        if causal_from is not None:
            ahead = iota((rows, rows), 0) <= iota((rows, rows), 1)
            last = jnp.where(ahead, scores[causal_from:, :], -BIG)
            if causal_from:
                scores = jnp.concatenate([scores[:causal_from, :], last], 0)
            else:
                scores = last
        weights = jnp.exp(scores - logsum(head))
        grad_weights = nt(values, own_grad)
        grad_scores = (weights * (grad_weights - col_sum(along[low:high]))).astype(BF)
        add_value(nn(weights.astype(BF), own_grad))
        add_key(nn(grad_scores, own_query))
        parts.append(nn(keys_t[low:high], grad_scores))
    parts.append(jnp.zeros((LANES - width, rows), F32))
    return jnp.concatenate(parts, 0).T


def split_values(values, width):
    rows = values.shape[0]
    zero = jnp.zeros((rows, LANES), BF)
    return [
        jnp.where(head_mask(rows, width, head), values, zero) for head in range(width // HEAD_DIM)
    ]


def transposed(values):
    return values.astype(F32).T.astype(BF)


def self_kernel(width, ids, ins, late, outs, saved, scratch):
    target, seg, bias = ins[:3]
    parts = ins[3:]
    keep_own, keep_x, send = outs
    place, rank = ids[0], ids[1]
    wide, state, lse_out = (item() for item in saved)
    q_out, k_out, v_out, mixed_out = (
        state.at[:, i * LANES : (i + 1) * LANES] for i in range(4)
    )
    place_padded(parts, place, wide)
    saved[0].flush()
    rows = target[...]
    length = rows.shape[0]
    block = length // 4
    segments = seg[...]
    q_out[...] = tag_queries((nn(rows, wide[:, :LANES]) + bias[0:1, :]) * 0.125, segments, width)
    k_out[...] = tag_keys(nn(rows, wide[:, LANES : 2 * LANES]), segments, width)
    v_out[...] = (nn(rows, wide[:, 2 * LANES : 3 * LANES]) + bias[1:2, :]).astype(BF)
    values = split_values(v_out[...], width)
    lse_out[...] = jnp.zeros_like(lse_out)
    for index in range(4):
        start, stop = index * block, (index + 1) * block

        def put_mixed(mixed):
            mixed_out[start:stop, :] = mixed

        def put_lse(head, row):
            lse_out[head : head + 1, start:stop] = row

        attend(
            q_out[start:stop, :],
            k_out[:stop, :],
            [value[:stop] for value in values],
            width,
            start,
            put_mixed,
            put_lse,
        )
    saved[1].flush()
    saved[2].flush()
    back = wide[:, 3 * LANES :]
    for hop in (3, 1, 2, 0):
        start = block_start(rank, block, 4, hop)
        part = nt(mixed_out[pl.ds(start, block), :], back)
        if hop == 0:
            keep_own[...] = part
        elif hop == 2:
            keep_x[...] = part
        else:
            send[hop // 2] = part.astype(BF)


def memory_kernel(width, ids, ins, late, outs, saved, scratch):
    memory, seg, bias = ins[:3]
    parts = ins[3:]
    wide, pair = (item() for item in saved)
    place = ids[0]
    rows = memory[...]
    segments = seg[...]
    for group in range(2):
        place_padded(parts, place, wide.at[group], group)
    saved[0].flush()
    for group in range(2):
        pair[group, :, :LANES] = tag_keys(
            nn(rows, wide[group, :, LANES : 2 * LANES]), segments, width
        )
        pair[group, :, LANES:] = (
            nn(rows, wide[group, :, 2 * LANES : 3 * LANES]) + bias[group, 3:4, :]
        ).astype(BF)


def first_norm_kernel(ids, ins, late, outs, saved, scratch):
    keep, from_core, from_x, target, rowv = ins
    low_out, first_out = outs
    xhat_out, scale_out = (item() for item in saved)
    summed = keep[...] + from_core[0].astype(F32) + from_x[...].astype(F32) + rowv[0:1, :]
    xhat, scale = normalize(target[...].astype(F32) + summed)
    xhat_out[...] = xhat
    scale_out[...] = jnp.broadcast_to(scale, scale_out.shape)
    first = xhat * rowv[3:4, :] + rowv[4:5, :]
    first_out[...] = first
    low_out[...] = first.astype(BF)


def cross_kernel(width, ids, ins, late, outs, saved, scratch):
    own, core, seg, bias = ins
    wide, pair = late
    keep, send = outs
    state, lse_out = (item() for item in saved)
    block = own.shape[0]
    lse_out[...] = jnp.zeros_like(lse_out)
    for hop, low in ((1, core), (0, own)):
        at = slice(hop * block, (hop + 1) * block)
        segments = seg[at, :]
        branch = jnp.zeros((block, own.shape[1]), F32)
        for group in range(2):
            queries = tag_queries(
                (nn(low[...], wide()[group, :, :LANES]) + bias[group, 2:3, :]) * 0.125,
                segments,
                width,
            )
            state[group, at, :LANES] = queries

            def put_mixed(mixed):
                state[group, at, LANES:] = mixed

            def put_lse(head, row):
                lse_out[group, head : head + 1, at] = row

            attend(
                queries,
                pair()[group, :, :LANES],
                split_values(pair()[group, :, LANES:], width),
                width,
                None,
                put_mixed,
                put_lse,
            )
            branch = branch + nt(state[group, at, LANES:], wide()[group, :, 3 * LANES :])
        if hop:
            send[...] = branch.astype(BF)
        else:
            keep[...] = branch


def second_norm_kernel(ids, ins, late, outs, saved, scratch):
    keep, from_core, first, rowv = ins
    low_out, second_out = outs
    xhat_out, scale_out = (item() for item in saved)
    summed = first[...] + (keep[...] + from_core[...].astype(F32) + rowv[1:2, :])
    xhat, scale = normalize(summed)
    xhat_out[...] = xhat
    scale_out[...] = jnp.broadcast_to(scale, scale_out.shape)
    second = xhat * rowv[5:6, :] + rowv[6:7, :]
    second_out[...] = second
    low_out[...] = second.astype(BF)


def gelu_both(values):
    bell = jnp.exp(-0.5 * values * values)
    inverse = 1.0 / (1.0 + 0.23164189 * jnp.abs(values))
    tail = inverse * (
        0.127414796
        + inverse
        * (
            -0.142248368
            + inverse * (0.7107068705 + inverse * (-0.7265760135 + inverse * 0.5307027145))
        )
    )
    tail = tail * bell
    area = jnp.where(values < 0.0, tail, 1.0 - tail)
    return values * area, area + values * bell * 0.3989422804


def ffn_rows(rows, expand, contract, bias):
    hidden, slope = gelu_both(nn(rows, expand) + bias)
    hidden = hidden.astype(BF)
    return hidden, slope.astype(BF), nt(hidden, contract)


def ffn_kernel(ids, ins, late, outs, saved, scratch):
    own, core, bias = ins[:3]
    if len(outs) > 4:
        expand, contract, hidden_out, slope_out, keep, send = outs
        parts = ins[3:]
        place_plain(parts, ids[0], expand, 0)
        place_plain(parts, ids[0], contract, 1)
    else:
        expand, contract = ins[3:]
        hidden_out, slope_out, keep, send = outs
    block = own.shape[0]
    for hop, rows, out in ((1, core, send), (0, own, keep)):
        at = slice(hop * block, (hop + 1) * block)
        hidden, slope, part = ffn_rows(rows[...], expand[...], contract[...], bias[...])
        hidden_out[at, :] = hidden
        slope_out[at, :] = slope
        out[...] = part.astype(out.dtype)


def last_norm_kernel(ids, ins, late, outs, saved, scratch):
    keep, from_core, from_x, second, cotangent, rowv = ins
    output, low_out, grad_out, sums = outs
    summed = keep[...] + from_core[...].astype(F32) + from_x[...].astype(F32) + rowv[2:3, :]
    xhat, scale = normalize(second[...] + summed)
    output[...] = (xhat * rowv[7:8, :] + rowv[8:9, :]).astype(BF)
    grad = cotangent[...].astype(F32)
    back = norm_back(grad, xhat, scale, rowv[7:8, :])
    grad_out[...] = back
    low = back.astype(BF)
    low_out[...] = low
    put_sums(sums, low, grad, xhat)


def put_sums(sums, low, grad, normed):
    sums[...] = jnp.zeros_like(sums)
    sums[0:1, :] = col_sum(low.astype(F32))
    sums[1:2, :] = col_sum(grad * normed)
    sums[2:3, :] = col_sum(grad)


def ffn_back_kernel(ids, ins, late, outs, saved, scratch):
    own, core, expand, contract, slope = ins
    pre_out, keep, send = outs
    block = own.shape[0]
    for hop, rows, out in ((1, core, send), (0, own, keep)):
        at = slice(hop * block, (hop + 1) * block)
        grad = (slope[at, :].astype(F32) * nn(rows[...], contract[...])).astype(BF)
        pre_out[at, :] = grad
        out[...] = nt(grad, expand[...]).astype(out.dtype)


def put_blocks(total, place, outs, hops, pack=None):
    if len(outs[0].shape) < 4 - len(outs[1:]):
        if pack is None:
            outs[0][...] = total[...].astype(BF)
        else:
            outs[0][pack] = total[...].astype(BF)
        return
    rows = outs[0].shape[-2]
    level = jnp.right_shift(place, 1)
    for step in range(4):
        for side in range(2):
            index = 2 * (jnp.bitwise_xor(level, step) if hops else step)
            if len(outs) == 2:
                index = index + jnp.bitwise_xor(jnp.bitwise_and(place, 1), side)
                out = outs[side].at[step]
            else:
                index = index + side
                out = outs[0].at[side, step]
            if not isinstance(index, int):
                index = pl.multiple_of(index * rows, rows)
            else:
                index = index * rows
            value = total[pl.ds(index, rows), :].astype(BF)
            if pack is None:
                out[...] = value
            else:
                out[pack] = value


def ffn_grad_kernel(ids, ins, late, outs, saved, scratch):
    rows, grads = ins[:4], ins[4:8]
    hidden_near, hidden_far, pre_near, pre_far = ins[8:]
    (total,) = scratch
    sums, keep = outs
    place = ids[0]
    block = rows[0].shape[0]

    def half(ref, hop):
        return ref[(hop % 2) * block : (hop % 2 + 1) * block, :]

    sums[...] = jnp.zeros_like(sums)
    sums[0:1, :] = col_sum(pre_near[...].astype(F32)) + col_sum(pre_far[...].astype(F32))
    for which, left, near, far in ((1, grads, hidden_near, hidden_far), (0, rows, pre_near, pre_far)):
        for hop in range(4):
            part = tn(left[hop][...], half(far if hop // 2 else near, hop))
            if hop == 0:
                total[...] = part
            else:
                total[...] += part
        put_blocks(total, place, [keep], False, which)


def second_back_kernel(ids, ins, late, outs, saved, scratch):
    keep, from_core, from_x, grad3, rowv = ins
    xhat, scale = late
    low_out, grad_out, sums = outs
    grad = grad3[...] + keep[...] + from_core[...].astype(F32) + from_x[...].astype(F32)
    normed = xhat()[...]
    grad2 = norm_back(grad, normed, scale()[:, 0:1], rowv[5:6, :])
    grad_out[...] = grad2
    low = grad2.astype(BF)
    low_out[...] = low
    put_sums(sums, low, grad, normed)


def first_back_kernel(ids, ins, late, outs, saved, scratch):
    keep, from_core, grad2, rowv = ins
    xhat, scale = late
    low_out, grad_out, sums = outs
    grad = grad2[...] + keep[...] + from_core[...].astype(F32)
    normed = xhat()[...]
    grad1 = norm_back(grad, normed, scale()[:, 0:1], rowv[3:4, :])
    grad_out[...] = grad1
    low = grad1.astype(BF)
    low_out[...] = low
    put_sums(sums, low, grad, normed)


def cross_back_kernel(width, ids, ins, late, outs, saved, scratch):
    own, core = ins
    wide, pair, state, lse = late
    dq_out, dk_out, dv_out, keep, send, bias_sums = outs
    dk_acc, dv_acc = scratch
    block = own.shape[0]
    bias_sums[...] = jnp.zeros_like(bias_sums)
    dk_acc[...] = jnp.zeros_like(dk_acc)
    dv_acc[...] = jnp.zeros_like(dv_acc)
    keys_t = None
    for hop, low in ((1, core), (0, own)):
        at = slice(hop * block, (hop + 1) * block)
        total = jnp.zeros((block, own.shape[1]), F32)
        if keys_t is None:
            keys_t = [transposed(pair()[group, :, :LANES]) for group in range(2)]
        for group in range(2):
            grad_mixed = nn(low[...], wide()[group, :, 3 * LANES :]).astype(BF)

            def add_key(value):
                dk_acc[group] += value

            def add_value(value):
                dv_acc[group] += value

            dq = attend_back(
                state()[group, at, :LANES],
                pair()[group, :, :LANES],
                pair()[group, :, LANES:],
                keys_t[group],
                grad_mixed,
                state()[group, at, LANES:],
                lambda head: lse()[group, head : head + 1, at],
                width,
                None,
                add_key,
                add_value,
            )
            dq_low = (dq.astype(BF).astype(F32) * 0.125).astype(BF)
            dq_out[group, at, :] = dq_low
            bias_sums[group, 0:1, :] += col_sum(dq_low.astype(F32))
            total = total + nt(dq_low, wide()[group, :, :LANES])
        if hop:
            send[...] = total.astype(BF)
        else:
            keep[...] = total
    for group in range(2):
        dk_out[group] = dk_acc[group].astype(BF)
        dv_low = dv_acc[group].astype(BF)
        dv_out[group] = dv_low
        bias_sums[group, 1:2, :] = col_sum(dv_low.astype(F32))


def cross_grad_kernel(width, ids, ins, late, outs, saved, scratch):
    dq, dk, dv, low_two, low_two_core, low1, low1_core = ins
    wide, state, memory = late
    (total,) = scratch
    mem_keep, mem_x, mem_send = outs[:3]
    place, rank = ids[0], ids[1]
    block = mem_keep.shape[0]
    rows = low1.shape[0]
    for group in range(2):
        total[:, 3 * width :] = (
            tn(low_two[...], state()[group, :rows, LANES:])
            + tn(low_two_core[...], state()[group, rows:, LANES:])
        )[:, :width]
        total[:, :width] = (
            tn(low1[...], dq[group, :rows, :]) + tn(low1_core[...], dq[group, rows:, :])
        )[:, :width]
        total[:, width : 2 * width] = tn(memory()[...], dk[group])[:, :width]
        total[:, 2 * width : 3 * width] = tn(memory()[...], dv[group])[:, :width]
        put_blocks(total, place, outs[3:], True, group)
    for hop in (1, 3, 2, 0):
        start = block_start(rank, block, 4, hop)
        part = jnp.zeros((block, wide().shape[1]), F32)
        for group in range(2):
            part = part + nt(dk[group, pl.ds(start, block), :], wide()[group, :, LANES : 2 * LANES])
            part = part + nt(
                dv[group, pl.ds(start, block), :], wide()[group, :, 2 * LANES : 3 * LANES]
            )
        if hop == 0:
            mem_keep[...] = part
        elif hop == 2:
            mem_x[...] = part
        else:
            mem_send[hop // 2] = part.astype(BF)


def self_back_kernel(width, ids, ins, late, outs, saved, scratch):
    grads = ins
    wide, state, lse, target = late
    low, total, dk_acc, dv_acc = scratch
    three, bias_sums = outs[:2]
    keeps = outs[2:]
    place, rank = ids[0], ids[1]
    length = low.shape[0]
    block = length // 4
    place_plain(grads, rank, low)
    grad_mixed = nn(low[...], wide()[:, 3 * LANES :]).astype(BF)
    q_in, k_in, v_in, mixed = (state().at[:, i * LANES : (i + 1) * LANES] for i in range(4))
    keys_t = transposed(k_in[...])
    dk_acc[...] = jnp.zeros_like(dk_acc)
    dv_acc[...] = jnp.zeros_like(dv_acc)
    bias_sums[...] = jnp.zeros_like(bias_sums)
    for index in range(4):
        start, stop = index * block, (index + 1) * block

        def add_key(value):
            dk_acc[:stop, :] += value

        def add_value(value):
            dv_acc[:stop, :] += value

        dq = attend_back(
            q_in[start:stop, :],
            k_in[:stop, :],
            v_in[:stop, :],
            keys_t[:, :stop],
            grad_mixed[start:stop],
            mixed[start:stop, :],
            lambda head: lse()[head : head + 1, start:stop],
            width,
            start,
            add_key,
            add_value,
        )
        three[start:stop, :LANES] = (dq.astype(BF).astype(F32) * 0.125).astype(BF)
    three[:, LANES : 2 * LANES] = dk_acc[...].astype(BF)
    three[:, 2 * LANES :] = dv_acc[...].astype(BF)
    bias_sums[0:1, :] = col_sum(three[:, :LANES].astype(F32))
    bias_sums[1:2, :] = col_sum(three[:, 2 * LANES :].astype(F32))
    part = tn(target()[...], three[...])
    for group in range(3):
        total[:, group * width : (group + 1) * width] = part[
            :, group * LANES : group * LANES + width
        ]
    total[:, 3 * width :] = tn(low[...], mixed[...])[:, :width]
    put_blocks(total, place, keeps, True)


def target_kernel(ids, ins, late, outs, saved, scratch):
    (three,) = ins
    (wide,) = late
    keep, keep_x, send = outs
    rank = ids[1]
    block = keep.shape[0]
    for hop in (3, 1, 2, 0):
        start = block_start(rank, block, 4, hop)
        part = nt(three[pl.ds(start, block), :], wide()[:, : 3 * LANES])
        if hop == 0:
            keep[...] = part
        elif hop == 2:
            keep_x[...] = part
        else:
            send[hop // 2] = part.astype(BF)


def join_kernel(ids, ins, late, outs, saved, scratch):
    rank = ids[1]
    block = ins[0].shape[0]
    for hop, part in enumerate(ins):
        outs[0][pl.ds(block_start(rank, block, 4, hop), block), :] = part[...].astype(outs[0].dtype)


def adam(weight, gradient, moment, square, rate, clip_scale):
    clipped = gradient * clip_scale
    new_moment = BETA_ONE * moment + (1.0 - BETA_ONE) * clipped
    new_square = BETA_TWO * square + (1.0 - BETA_TWO) * clipped * clipped
    fixed_moment = new_moment / (1.0 - BETA_ONE**STEP)
    fixed_square = new_square / (1.0 - BETA_TWO**STEP)
    new_weight = weight - rate * (
        fixed_moment / (jnp.sqrt(fixed_square) + ADAM_EPS) + DECAY * weight
    )
    return (new_weight, new_moment, new_square)


def adam_kernel(width, ids, ins, late, outs, saved, scratch):
    squares, own, cross, expand, contract, small = ins[:6]
    leaves = [ins[6 + 3 * i : 9 + 3 * i] for i in range(7)]
    norm = jnp.sqrt(squares[0:1, 0:1])
    outs[0][...] = jnp.broadcast_to(norm, outs[0].shape)
    scale = jnp.minimum(1.0, MAX_NORM / (norm + 1e-06))

    def update(leaf, index, at, gradient, rate):
        weight, moment, square = (ref[at] for ref in leaf)
        new = adam(weight, gradient, moment, square, rate, scale)
        first = 1 + 4 * index if index < 4 else 17 + 3 * (index - 4)
        for i in range(3):
            outs[first + i][at] = new[i]
        if index < 4:
            outs[first + 3][at] = new[0].astype(BF)

    everything = (slice(None), slice(None))
    for half, pack in enumerate((own, cross)):
        for i in range(3):
            part = pack[:, i * width : (i + 1) * width]
            update(leaves[0], 0, 3 * half + i, part, RATE_MATRIX)
        update(leaves[1], 1, half, pack[:, 3 * width :].T, RATE_MATRIX)
    update(leaves[2], 2, everything, expand[...], RATE_MATRIX)
    update(leaves[3], 3, everything, contract[...], RATE_MATRIX)
    for i in range(4):
        at = (slice(i, i + 1), slice(None))
        update(leaves[4], 4, at, small[9:10, i * width : (i + 1) * width], RATE_VECTOR)
    update(leaves[5], 5, everything, small[10:11, :], RATE_VECTOR)
    update(leaves[6], 6, everything, small[0:9, :], RATE_VECTOR)


def local(
    data_size,
    tensor_size,
    target,
    memory,
    target_segments,
    memory_segments,
    cotangent,
    input_weights,
    input_moment,
    input_square,
    output_weights,
    output_moment,
    output_square,
    expand_weights,
    expand_moment,
    expand_square,
    contract_weights,
    contract_moment,
    contract_square,
    head_biases,
    head_moment,
    head_square,
    hidden_biases,
    hidden_moment,
    hidden_square,
    row_vectors,
    row_moment,
    row_square,
):
    length, model = target.shape[1:]
    mem_length = memory.shape[1]
    width = head_biases.shape[1]
    block = length // tensor_size
    mem_block = mem_length // tensor_size
    share = model // data_size
    direct = data_size == 8 and share % 16 == 0
    place = lax.axis_index("dp")
    rank = lax.axis_index("tensor")
    ids = jnp.stack([place, rank]).astype(jnp.int32)
    target_rows = target.reshape(length, model)
    memory_rows = memory.reshape(mem_length, model)
    cotangent_rows = cotangent.reshape(length, model)
    target_seg = target_segments.reshape(length, 1)
    memory_seg = memory_segments.reshape(mem_length, 1)
    rowv = jnp.pad(row_vectors, ((0, 7), (0, 0)))
    bias = jnp.pad(head_biases, ((0, 4), (0, LANES - width)))

    def to_tensor(value, hop):
        return lax.ppermute(value, "tensor", [(i, i ^ hop) for i in range(tensor_size)])

    def to_data(value, hop):
        return lax.ppermute(value, "dp", [(i, i ^ hop) for i in range(data_size)])

    def over_z(value):
        groups = [list(range(side, data_size, 2)) for side in range(2)]
        return lax.all_to_all(value, "dp", 0, 0, axis_index_groups=groups, tiled=True)

    def gather_plain(value):
        return [lax.all_gather(value, "dp", axis=value.ndim - 2, tiled=True)]

    def spread(value):
        return over_z(jnp.broadcast_to(value[None], (4,) + value.shape))

    def over_y(value):
        groups = [[side, side + 1] for side in range(0, data_size, 2)]
        return lax.all_to_all(value, "dp", 0, 0, axis_index_groups=groups, tiled=True)

    def added(received):
        return (received[0].astype(F32) + received[1].astype(F32)).astype(BF)

    def hops_z(value):
        return [value[0]] + [to_data(value[hop], 2 * hop) for hop in (1, 2, 3)]

    def total_of(received):
        first, second, third, fourth = (part.astype(F32) for part in received)
        return (first + second) + (third + fourth)

    def scatter_plain(value):
        return lax.psum_scatter(
            value, "dp", scatter_dimension=value.ndim - 2, tiled=True
        ).astype(F32)

    def sum_data(value):
        if not direct:
            return lax.psum(value, "dp")
        value = value + to_data(value, 1)
        got = [to_data(value, hop) for hop in (2, 4, 6)]
        return (value + got[0]) + (got[1] + got[2])

    def join(own, far, dtype):
        core = to_tensor(own, 1)
        diag = to_tensor(far, 1)
        rows = own.shape[0] * 4
        return call(
            join_kernel, ids, [own, core, far, diag], [], [SDS((rows, model), dtype)], [], name="join"
        )[0]

    def sum_rows(keep_x, send_x):
        return (keep_x + send_x.astype(F32)).astype(BF)

    self_pack = jnp.concatenate(
        [input_weights[0], input_weights[1], input_weights[2], output_weights[0].T], axis=1
    ).astype(BF)
    cross_pack = jnp.concatenate(
        [input_weights[3], input_weights[4], input_weights[5], output_weights[1].T], axis=1
    ).astype(BF)
    cross_far = to_tensor(cross_pack, 2)
    bias_far = to_tensor(bias, 2)
    target_own = lax.dynamic_slice_in_dim(target_rows, rank * block, block, 0)
    cotangent_own = lax.dynamic_slice_in_dim(cotangent_rows, rank * block, block, 0)
    seg_near = jnp.concatenate(
        [
            lax.dynamic_slice_in_dim(target_seg, (rank ^ hop) * block, block, 0)
            for hop in range(2)
        ]
    )
    cross_pair = jnp.stack([cross_pack, cross_far])
    ffn_pair = jnp.stack([expand_weights.astype(BF), contract_weights.T.astype(BF)])
    if direct:
        self_z = [to_data(self_pack, hop) for hop in (2, 4, 6)]
        self_parts = [self_pack, to_data(self_pack, 1)]
        for part in self_z:
            self_parts += [part, to_data(part, 1)]
        cross_parts = [spread(cross_pair)]
        cross_parts.append(to_data(cross_parts[0], 1))
    else:
        self_parts, cross_parts = gather_plain(self_pack), gather_plain(cross_pair)
    cross_bias = jnp.stack([bias, bias_far])

    quarter = SDS((block, model), F32)
    quarter_low = SDS((block, model), BF)
    pair_low = SDS((2, block, model), BF)
    column = SDS((block, 128), F32)
    sums_shape = SDS((8, model), F32)
    padded = 4 * LANES

    (keep, keep_x, send, wide_self, state_self, lse_self) = call(
        partial(self_kernel, width),
        ids,
        [target_rows, target_seg, bias, *self_parts],
        [],
        [quarter, quarter, pair_low],
        [SDS((model, padded), BF), SDS((length, padded), BF), SDS((8, length), F32)],
        flops=2 * length * model * padded + 8 * length * length * LANES,
        name="self_forward",
    )
    from_core = to_tensor(send, 1)
    to_far = sum_rows(keep_x, from_core[1])
    from_x = to_tensor(to_far, 2)
    if direct:
        ffn_parts = [spread(after(ffn_pair, to_far))]
        ffn_parts.append(to_data(ffn_parts[0], 1))
    else:
        ffn_parts = gather_plain(ffn_pair)

    mem_rows = SDS((2, mem_length, LANES), BF)
    wide_cross, kv_cross = call(
        partial(memory_kernel, width),
        ids,
        [memory_rows, memory_seg, cross_bias, *cross_parts],
        [],
        [],
        [SDS((2, model, padded), BF), SDS((2, mem_length, 2 * LANES), BF)],
        flops=8 * mem_length * model * LANES,
        name="memory_rows",
    )
    low1, first, xhat1, scale1 = call(
        first_norm_kernel,
        ids,
        [keep, from_core, from_x, target_own, rowv],
        [],
        [quarter_low, quarter],
        [quarter, column],
        name="first_norm",
    )
    low1_core = to_tensor(low1, 1)
    pair_rows = SDS((2, 2 * block, LANES), BF)
    keep, send, state_cross, lse_cross = call(
        partial(cross_kernel, width),
        ids,
        [low1, low1_core, seg_near, cross_bias],
        [wide_cross, kv_cross],
        [quarter, quarter_low],
        [SDS((2, 2 * block, 2 * LANES), BF), SDS((2, 8, 2 * block), F32)],
        flops=16 * block * model * LANES + 48 * block * mem_length * LANES,
        name="cross_forward",
    )
    low2, second, xhat2, scale2 = call(
        second_norm_kernel,
        ids,
        [keep, to_tensor(send, 1), first, rowv],
        [],
        [quarter_low, quarter],
        [quarter, column],
        name="second_norm",
    )

    low2_x = to_tensor(low2, 2)
    low2_core = to_tensor(low2, 1)
    hidden_row = hidden_biases.reshape(1, -1)
    units = hidden_row.shape[1]
    half_units = SDS((2 * block, units), BF)
    ffn_flops = 8 * block * model * units
    expand_all, contract_all, hidden_near, slope_near, keep, send = call(
        ffn_kernel,
        ids,
        [low2, low2_core, hidden_row, *ffn_parts],
        [],
        [SDS((model, units), BF)] * 2 + [half_units, half_units, quarter, quarter_low],
        [],
        flops=ffn_flops,
        name="ffn_near",
    )
    from_core = to_tensor(send, 1)
    low2_diag = to_tensor(low2_x, 1)
    hidden_far, slope_far, keep_x, send = call(
        ffn_kernel,
        ids,
        [low2_x, low2_diag, hidden_row, expand_all, contract_all],
        [],
        [half_units, half_units, quarter, quarter_low],
        [],
        flops=ffn_flops,
        name="ffn_far",
    )
    from_x = to_tensor(sum_rows(keep_x, to_tensor(send, 1)), 2)
    out_own, low3, grad3, sums3 = call(
        last_norm_kernel,
        ids,
        [keep, from_core, from_x, second, cotangent_own, rowv],
        [],
        [quarter_low, quarter_low, quarter, sums_shape],
        [],
        name="last_norm",
    )

    low3_x = to_tensor(low3, 2)
    low3_core = to_tensor(low3, 1)
    pre_near, keep, send = call(
        ffn_back_kernel,
        ids,
        [low3, low3_core, expand_all, contract_all, slope_near],
        [],
        [half_units, quarter, quarter_low],
        [],
        flops=ffn_flops,
        name="ffn_back_near",
    )
    from_core = to_tensor(send, 1)
    low3_diag = to_tensor(low3_x, 1)
    pre_far, keep_x, send = call(
        ffn_back_kernel,
        ids,
        [low3_x, low3_diag, expand_all, contract_all, slope_far],
        [],
        [half_units, quarter, quarter_low],
        [],
        flops=ffn_flops,
        name="ffn_back_far",
    )
    to_far = sum_rows(keep_x, to_tensor(send, 1))
    from_x = to_tensor(to_far, 2)
    blocks = [SDS((4, share, model), BF)] * 2 if direct else [SDS((model, model), BF)]
    pair = SDS((2, 4, 2, share, model), BF) if direct else SDS((2, model, model), BF)
    ffn_outs = call(
        ffn_grad_kernel,
        ids,
        [after(low2, to_far), low2_core, low2_x, low2_diag, low3, low3_core, low3_x, low3_diag]
        + [hidden_near, hidden_far, pre_near, pre_far],
        [],
        [SDS((8, units), F32)] + [pair],
        [],
        [pltpu.VMEM((model, units), F32)],
        flops=2 * ffn_flops,
        name="ffn_grad",
    )
    hidden_sums = ffn_outs[0]
    ffn_along = over_y(ffn_outs[1]) if direct else None

    low_two, grad2, sums2 = call(
        second_back_kernel,
        ids,
        [after(keep, ffn_outs[1]), from_core, from_x, grad3, rowv],
        [xhat2, scale2],
        [quarter_low, quarter, sums_shape],
        [],
        name="second_back",
    )
    low_two_core = to_tensor(low_two, 1)
    output_far = to_tensor(after(out_own, low_two), 2)
    dq, dk, dv, keep, send, bias_sums = call(
        partial(cross_back_kernel, width),
        ids,
        [low_two, low_two_core],
        [wide_cross, kv_cross, state_cross, lse_cross],
        [pair_rows, mem_rows, mem_rows, quarter, quarter_low, SDS((2, 8, LANES), F32)],
        [],
        [pltpu.VMEM((2, mem_length, LANES), F32)] * 2,
        flops=16 * block * model * LANES + 120 * block * mem_length * LANES,
        name="cross_back",
    )
    mem_quarter = SDS((mem_block, model), F32)
    cross_outs = call(
        partial(cross_grad_kernel, width),
        ids,
        [dq, dk, dv, low_two, low_two_core, low1, low1_core],
        [wide_cross, state_cross, memory_rows],
        [mem_quarter, mem_quarter, SDS((2, mem_block, model), BF)]
        + ([SDS((4, 2, share, model), BF)] * 2 if direct else [pair]),
        [],
        [pltpu.VMEM((model, model), F32)],
        flops=24 * mem_length * model * LANES,
        name="cross_grad",
    )
    mem_keep, mem_x, mem_send = cross_outs[:3]
    cross_along = to_data(cross_outs[4], 1) if direct else None

    low_one, grad1, sums1 = call(
        first_back_kernel,
        ids,
        [after(keep, cross_outs[0]), to_tensor(after(send, output_far), 1), grad2, rowv],
        [xhat1, scale1],
        [quarter_low, quarter, sums_shape],
        [],
        name="first_back",
    )
    low_one_x = to_tensor(low_one, 2)
    low_one_core = to_tensor(low_one, 1)
    if direct:
        ffn_received = over_z(added(ffn_along))
    low_one_diag = to_tensor(low_one_x, 1)

    back_outs = call(
        partial(self_back_kernel, width),
        ids,
        [low_one, low_one_core, low_one_x, low_one_diag],
        [wide_self, state_self, lse_self, target_rows],
        [SDS((length, 3 * LANES), BF), SDS((8, LANES), F32)] + blocks,
        [],
        [pltpu.VMEM((length, model), BF), pltpu.VMEM((model, model), F32)]
        + [pltpu.VMEM((length, LANES), F32)] * 2,
        flops=4 * length * model * padded + 20 * length * length * LANES,
        name="self_back",
    )
    three, self_sums, keep_self = back_outs[:3]
    if direct:
        self_along = to_data(back_outs[3], 1)
        late_rows = after(jnp.stack(
            [sums1[0], sums2[0], sums3[0], sums1[1], sums1[2], sums2[1], sums2[2], sums3[1], sums3[2]]
        ), self_along)
        cross_received = hops_z(added((cross_outs[3], cross_along)))
        self_received = hops_z(added((keep_self, self_along)))
        ffn_share = total_of(ffn_received)
        cross_both = total_of(cross_received)
        self_share = total_of(self_received)
    else:
        ffn_share = scatter_plain(ffn_outs[1])
        cross_both = scatter_plain(cross_outs[3])
        self_share = scatter_plain(keep_self)
        late_rows = jnp.stack(
            [sums1[0], sums2[0], sums3[0], sums1[1], sums1[2], sums2[1], sums2[2], sums3[1], sums3[2]]
        )
    cross_share = cross_both[0] + to_tensor(cross_both[1].astype(BF), 2).astype(F32)
    expand_share, contract_share = ffn_share[0], ffn_share[1]

    keep, keep_x, send = call(
        target_kernel,
        ids,
        [three],
        [wide_self],
        [quarter, quarter, pair_low],
        [],
        flops=6 * length * model * LANES,
        name="target_grad",
    )
    from_core = to_tensor(send, 1)
    from_x = to_tensor(sum_rows(keep_x, from_core[1]), 2)
    target_sum = (grad1 + keep + from_core[0].astype(F32) + from_x.astype(F32)).astype(BF)
    from_core = to_tensor(after(mem_send, three), 1)
    from_x = to_tensor(sum_rows(mem_x, from_core[1]), 2)
    memory_sum = (mem_keep + from_core[0].astype(F32) + from_x.astype(F32)).astype(BF)

    output = join(out_own, output_far, BF)
    memory_far = to_tensor(memory_sum, 2)
    memory_grad = join(memory_sum, memory_far, F32)
    target_far = to_tensor(target_sum, 2)
    target_grad = join(target_sum, target_far, F32)

    row_part = late_rows
    row_part = row_part + to_tensor(row_part, 1)
    row_part = row_part + to_tensor(row_part, 2)
    cross_sums = bias_sums[:, :2, :width]
    near = cross_sums[0] + to_tensor(cross_sums[1], 2)
    head_part = jnp.concatenate([self_sums[:2, :width], near], axis=0)
    small = sum_data(
        jnp.concatenate([row_part, head_part.reshape(1, -1), hidden_sums[:1]], axis=0)
    )
    row_grad = small[:9]
    head_grad = small[9].reshape(4, width)
    hidden_grad = small[10]

    own_squares = (
        jnp.sum(self_share * self_share)
        + jnp.sum(cross_share * cross_share)
        + jnp.sum(expand_share * expand_share)
        + jnp.sum(contract_share * contract_share)
    )
    shared_squares = (
        jnp.sum(head_grad * head_grad) + jnp.sum(hidden_grad * hidden_grad)
    ) / data_size
    common_squares = jnp.sum(row_grad * row_grad) / (data_size * tensor_size)
    squares = (own_squares + shared_squares + common_squares).reshape(1, 1)
    squares = after(squares, target_far, memory_far)
    squares = squares + to_tensor(squares, 1)
    squares = squares + to_tensor(squares, 2)
    squares = sum_data(squares)
    hidden = [value.reshape(1, -1) for value in (hidden_biases, hidden_moment, hidden_square)]
    leaves = [input_weights, input_moment, input_square, output_weights, output_moment]
    leaves += [output_square, expand_weights, expand_moment, expand_square]
    leaves += [value.T for value in (contract_weights, contract_moment, contract_square)]
    leaves += [head_biases, head_moment, head_square, *hidden]
    leaves += [row_vectors, row_moment, row_square]
    shapes = [SDS((1, 1), F32)]
    for i in range(7):
        shapes += [SDS(leaf.shape, F32) for leaf in leaves[3 * i : 3 * i + 3]]
        if i < 4:
            shapes.append(SDS(leaves[3 * i].shape, BF))
    new = call(
        partial(adam_kernel, width),
        ids,
        [squares, self_share, cross_share, expand_share, contract_share, small, *leaves],
        [],
        shapes,
        [],
        name="adam",
    )
    return (
        output.reshape(target.shape),
        target_grad.reshape(target.shape),
        memory_grad.reshape(memory.shape),
        new[0][0, 0],
        *new[1:13],
        *(value.T for value in new[13:17]),
        *new[17:20],
        *(value.reshape(-1) for value in new[20:23]),
        *new[23:],
    )


def solution(mesh):
    rows = P("dp", None, None)
    in_matrix = P(None, "dp", "tensor")
    out_matrix = P(None, "tensor", "dp")
    return jax.shard_map(
        partial(local, mesh.shape["dp"], mesh.shape["tensor"]),
        mesh=mesh,
        in_specs=(rows, rows, P("dp", None), P("dp", None), rows)
        + (in_matrix,) * 3
        + (out_matrix,) * 3
        + (P("dp", "tensor"),) * 3
        + (P("tensor", "dp"),) * 3
        + (P(None, "tensor"),) * 3
        + (P("tensor"),) * 3
        + (P(),) * 3,
        out_specs=(rows, rows, rows, P())
        + (in_matrix,) * 4
        + (out_matrix,) * 4
        + (P("dp", "tensor"),) * 4
        + (P("tensor", "dp"),) * 4
        + (P(None, "tensor"),) * 3
        + (P("tensor"),) * 3
        + (P(),) * 3,
        check_vma=False,
    )
```

```python
from functools import partial

import jax
import jax.numpy as jnp
from jax import lax
from jax.experimental import pallas as pl
from jax.experimental.pallas import tpu as pltpu
from jax.sharding import PartitionSpec as P

HEAD_DIM = 64
STEP = 10
NORM_EPS = 1e-05
BETA_ONE = 0.9
BETA_TWO = 0.999
RATE_MATRIX = 0.06
RATE_VECTOR = 0.5
DECAY = 0.01
ADAM_EPS = 1e-08
MAX_NORM = 1.0
BIG = 1e30
LANES = 256
MIB = 2**20
COST = 1.0

BF = jnp.bfloat16
F32 = jnp.float32
SDS = jax.ShapeDtypeStruct


def nn(left, right):
    return jnp.dot(left, right, preferred_element_type=F32)


def nt(left, right):
    return lax.dot_general(left, right, (((1,), (1,)), ((), ())), preferred_element_type=F32)


def tn(left, right):
    return lax.dot_general(left, right, (((0,), (0,)), ((), ())), preferred_element_type=F32)


def iota(shape, dim):
    return lax.broadcasted_iota(jnp.int32, shape, dim)


class Late:
    def __init__(self, copy, buffer):
        self.copy, self.buffer, self.waited = copy, buffer, False

    def __call__(self):
        if not self.waited:
            self.copy.wait()
            self.waited = True
        return self.buffer


class Saved:
    def __init__(self, copy, buffer):
        self.copy, self.buffer, self.started = copy, buffer, False

    def __call__(self):
        return self.buffer

    def flush(self):
        self.copy.start()
        self.started = True


def call(body, ids, ins, late, outs, saved, scratch=(), flops=0, vmem=32, name=None):
    counts = [len(ins), len(late), len(outs), len(saved), len(late), len(saved), len(scratch)]

    def kernel(ids_ref, *refs):
        groups = []
        start = 0
        for number in counts:
            groups.append(refs[start : start + number])
            start += number
        in_refs, late_refs, out_refs, saved_refs, late_bufs, saved_bufs, extra = groups
        sems = refs[start] if late or saved else None
        lates = [
            Late(pltpu.make_async_copy(ref, buf, sems.at[i]), buf)
            for i, (ref, buf) in enumerate(zip(late_refs, late_bufs))
        ]
        for item in lates:
            item.copy.start()
        saves = [
            Saved(pltpu.make_async_copy(buf, ref, sems.at[len(late) + i]), buf)
            for i, (ref, buf) in enumerate(zip(saved_refs, saved_bufs))
        ]
        body(ids_ref, in_refs, lates, out_refs, saves, extra)
        for item in lates:
            item()
        for item in saves:
            if not item.started:
                item.flush()
        for item in saves:
            item.copy.wait()

    size = sum(a.size * a.dtype.itemsize for a in [*ins, *late])
    size += sum(o.size * o.dtype.itemsize for o in [*outs, *saved])
    vmem_spec = pl.BlockSpec(memory_space=pltpu.VMEM)
    hbm_spec = pl.BlockSpec(memory_space=pltpu.HBM)
    sems = [pltpu.SemaphoreType.DMA((len(late) + len(saved),))] if late or saved else []
    result = pl.pallas_call(
        kernel,
        out_shape=[*outs, *saved],
        in_specs=[pl.BlockSpec(memory_space=pltpu.SMEM)]
        + [vmem_spec] * len(ins)
        + [hbm_spec] * len(late),
        out_specs=[vmem_spec] * len(outs) + [hbm_spec] * len(saved),
        scratch_shapes=[pltpu.VMEM(a.shape, a.dtype) for a in [*late, *saved]]
        + list(scratch)
        + sems,
        compiler_params=pltpu.CompilerParams(vmem_limit_bytes=vmem * MIB),
        cost_estimate=pl.CostEstimate(
            flops=int(flops * COST), bytes_accessed=int(size * COST), transcendentals=0
        ),
        name=name,
    )(ids, *ins, *late)
    return result


def after(value, *others):
    if not others:
        return value
    return lax.optimization_barrier((value, *others))[0]


def block_start(index, rows, blocks, hop):
    if blocks == 1:
        return 0
    return pl.multiple_of(jnp.bitwise_xor(index, hop) * rows, rows)


def pieces(parts, place, pack):
    if len(parts) == 2:
        side = jnp.bitwise_and(place, 1)
        rows = parts[0].shape[2]
        for half, part in enumerate(parts):
            for level in range(4):
                index = 2 * level + jnp.bitwise_xor(side, half)
                yield part.at[level, pack], pl.multiple_of(index * rows, rows)
    else:
        for hop, part in enumerate(parts):
            block = part if pack is None else part.at[pack]
            rows = block.shape[0]
            yield block, block_start(place, rows, len(parts), hop)


def place_padded(parts, place, out, pack=None):
    width = parts[0].shape[-1] // 4
    for group in range(4):
        out[:, group * LANES + width : (group + 1) * LANES] = jnp.zeros(
            (out.shape[0], LANES - width), BF
        )
    for part, start in pieces(parts, place, pack):
        for group in range(4):
            out[pl.ds(start, part.shape[0]), group * LANES : group * LANES + width] = part[
                :, group * width : (group + 1) * width
            ]


def place_plain(parts, place, out, pack=None):
    for part, start in pieces(parts, place, pack):
        out[pl.ds(start, part.shape[0]), :] = part[...]


def normalize(values):
    center = jnp.mean(values, axis=-1, keepdims=True)
    centered = values - center
    spread = jnp.mean(centered * centered, axis=-1, keepdims=True)
    scale_row = lax.rsqrt(spread + NORM_EPS)
    return centered * scale_row, scale_row


def norm_back(grad_out, normed, scale_row, gain):
    scaled = grad_out * gain
    return scale_row * (
        scaled
        - jnp.mean(scaled, axis=-1, keepdims=True)
        - normed * jnp.mean(scaled * normed, axis=-1, keepdims=True)
    )


def col_sum(values):
    return jnp.sum(values, axis=0, keepdims=True)


def head_mask(rows, width, head):
    lane = iota((rows, LANES), 1)
    return (lane >= head * HEAD_DIM) & (lane < (head + 1) * HEAD_DIM)


def tag_queries(queries, seg, width):
    doc = iota(queries.shape, 1) - width
    tagged = (doc >= 0) & (doc < 4)
    return jnp.where(tagged, jnp.where(doc == seg, 0.0, -BIG), queries).astype(BF)


def tag_keys(keys, seg, width):
    doc = iota(keys.shape, 1) - width
    return jnp.where(doc == seg, 1.0, keys).astype(BF)


def attend(queries, keys, values, width, causal_from, mixed_out, logsum_out):
    rows = queries.shape[0]
    count = keys.shape[0]
    lane = iota((rows, LANES), 1)
    mixed = jnp.zeros((rows, LANES), F32)
    for head in range(width // HEAD_DIM):
        mask = head_mask(rows, width, head) | (lane >= width)
        scores = nt(jnp.where(mask, queries, jnp.zeros_like(queries)), keys)
        if causal_from is not None:
            ahead = iota((rows, rows), 1) <= iota((rows, rows), 0)
            last = jnp.where(ahead, scores[:, causal_from:], -BIG)
            if causal_from:
                scores = jnp.concatenate([scores[:, :causal_from], last], 1)
            else:
                scores = last
        top = jnp.max(scores, axis=1, keepdims=True)
        weights = jnp.exp(scores - top)
        total = jnp.sum(weights, axis=1, keepdims=True)
        mixed = mixed + nn(weights.astype(BF), values[head]) * (1.0 / total)
        logsum_out(head, (top + jnp.log(total)).reshape(1, rows))
    mixed_out(mixed.astype(BF))


def attend_back(queries, keys, values, keys_t, grad, mixed, logsum, width, causal_from, add_key, add_value):
    rows = queries.shape[0]
    lane = iota((rows, LANES), 1)
    along = (grad.astype(F32) * mixed.astype(F32)).T
    parts = []
    zero = jnp.zeros_like(queries)
    for head in range(width // HEAD_DIM):
        low, high = head * HEAD_DIM, (head + 1) * HEAD_DIM
        mask = head_mask(rows, width, head)
        own_query = jnp.where(mask, queries, zero)
        own_grad = jnp.where(mask, grad, zero)
        scores = nt(keys, jnp.where(lane >= width, queries, own_query))
        if causal_from is not None:
            ahead = iota((rows, rows), 0) <= iota((rows, rows), 1)
            last = jnp.where(ahead, scores[causal_from:, :], -BIG)
            if causal_from:
                scores = jnp.concatenate([scores[:causal_from, :], last], 0)
            else:
                scores = last
        weights = jnp.exp(scores - logsum(head))
        grad_weights = nt(values, own_grad)
        grad_scores = (weights * (grad_weights - col_sum(along[low:high]))).astype(BF)
        add_value(nn(weights.astype(BF), own_grad))
        add_key(nn(grad_scores, own_query))
        parts.append(nn(keys_t[low:high], grad_scores))
    parts.append(jnp.zeros((LANES - width, rows), F32))
    return jnp.concatenate(parts, 0).T


def split_values(values, width):
    rows = values.shape[0]
    zero = jnp.zeros((rows, LANES), BF)
    return [
        jnp.where(head_mask(rows, width, head), values, zero) for head in range(width // HEAD_DIM)
    ]


def transposed(values):
    return values.astype(F32).T.astype(BF)


def self_kernel(width, ids, ins, late, outs, saved, scratch):
    target, seg, bias = ins[:3]
    parts = ins[3:]
    keep_own, keep_x, send = outs
    place, rank = ids[0], ids[1]
    wide, state, lse_out = (item() for item in saved)
    q_out, k_out, v_out, mixed_out = (
        state.at[:, i * LANES : (i + 1) * LANES] for i in range(4)
    )
    place_padded(parts, place, wide)
    saved[0].flush()
    rows = target[...]
    length = rows.shape[0]
    block = length // 4
    segments = seg[...]
    q_out[...] = tag_queries((nn(rows, wide[:, :LANES]) + bias[0:1, :]) * 0.125, segments, width)
    k_out[...] = tag_keys(nn(rows, wide[:, LANES : 2 * LANES]), segments, width)
    v_out[...] = (nn(rows, wide[:, 2 * LANES : 3 * LANES]) + bias[1:2, :]).astype(BF)
    values = split_values(v_out[...], width)
    lse_out[...] = jnp.zeros_like(lse_out)
    for index in range(4):
        start, stop = index * block, (index + 1) * block

        def put_mixed(mixed):
            mixed_out[start:stop, :] = mixed

        def put_lse(head, row):
            lse_out[head : head + 1, start:stop] = row

        attend(
            q_out[start:stop, :],
            k_out[:stop, :],
            [value[:stop] for value in values],
            width,
            start,
            put_mixed,
            put_lse,
        )
    saved[1].flush()
    saved[2].flush()
    back = wide[:, 3 * LANES :]
    for hop in (3, 1, 2, 0):
        start = block_start(rank, block, 4, hop)
        part = nt(mixed_out[pl.ds(start, block), :], back)
        if hop == 0:
            keep_own[...] = part
        elif hop == 2:
            keep_x[...] = part
        else:
            send[hop // 2] = part.astype(BF)


def memory_kernel(width, ids, ins, late, outs, saved, scratch):
    memory, seg, bias = ins[:3]
    parts = ins[3:]
    wide, pair = (item() for item in saved)
    place = ids[0]
    rows = memory[...]
    segments = seg[...]
    for group in range(2):
        place_padded(parts, place, wide.at[group], group)
    saved[0].flush()
    for group in range(2):
        pair[group, :, :LANES] = tag_keys(
            nn(rows, wide[group, :, LANES : 2 * LANES]), segments, width
        )
        pair[group, :, LANES:] = (
            nn(rows, wide[group, :, 2 * LANES : 3 * LANES]) + bias[group, 3:4, :]
        ).astype(BF)


def first_norm_kernel(ids, ins, late, outs, saved, scratch):
    keep, from_core, from_x, target, rowv = ins
    low_out, first_out = outs
    xhat_out, scale_out = (item() for item in saved)
    summed = keep[...] + from_core[0].astype(F32) + from_x[...].astype(F32) + rowv[0:1, :]
    xhat, scale = normalize(target[...].astype(F32) + summed)
    xhat_out[...] = xhat
    scale_out[...] = jnp.broadcast_to(scale, scale_out.shape)
    first = xhat * rowv[3:4, :] + rowv[4:5, :]
    first_out[...] = first
    low_out[...] = first.astype(BF)


def cross_kernel(width, ids, ins, late, outs, saved, scratch):
    own, core, seg, bias = ins
    wide, pair = late
    keep, send = outs
    state, lse_out = (item() for item in saved)
    block = own.shape[0]
    lse_out[...] = jnp.zeros_like(lse_out)
    for hop, low in ((1, core), (0, own)):
        at = slice(hop * block, (hop + 1) * block)
        segments = seg[at, :]
        branch = jnp.zeros((block, own.shape[1]), F32)
        for group in range(2):
            queries = tag_queries(
                (nn(low[...], wide()[group, :, :LANES]) + bias[group, 2:3, :]) * 0.125,
                segments,
                width,
            )
            state[group, at, :LANES] = queries

            def put_mixed(mixed):
                state[group, at, LANES:] = mixed

            def put_lse(head, row):
                lse_out[group, head : head + 1, at] = row

            attend(
                queries,
                pair()[group, :, :LANES],
                split_values(pair()[group, :, LANES:], width),
                width,
                None,
                put_mixed,
                put_lse,
            )
            branch = branch + nt(state[group, at, LANES:], wide()[group, :, 3 * LANES :])
        if hop:
            send[...] = branch.astype(BF)
        else:
            keep[...] = branch


def second_norm_kernel(ids, ins, late, outs, saved, scratch):
    keep, from_core, first, rowv = ins
    low_out, second_out = outs
    xhat_out, scale_out = (item() for item in saved)
    summed = first[...] + (keep[...] + from_core[...].astype(F32) + rowv[1:2, :])
    xhat, scale = normalize(summed)
    xhat_out[...] = xhat
    scale_out[...] = jnp.broadcast_to(scale, scale_out.shape)
    second = xhat * rowv[5:6, :] + rowv[6:7, :]
    second_out[...] = second
    low_out[...] = second.astype(BF)


def gelu_both(values):
    bell = jnp.exp(-0.5 * values * values)
    inverse = 1.0 / (1.0 + 0.23164189 * jnp.abs(values))
    tail = inverse * (
        0.127414796
        + inverse
        * (
            -0.142248368
            + inverse * (0.7107068705 + inverse * (-0.7265760135 + inverse * 0.5307027145))
        )
    )
    tail = tail * bell
    area = jnp.where(values < 0.0, tail, 1.0 - tail)
    return values * area, area + values * bell * 0.3989422804


def ffn_rows(rows, expand, contract, bias):
    hidden, slope = gelu_both(nn(rows, expand) + bias)
    hidden = hidden.astype(BF)
    return hidden, slope.astype(BF), nt(hidden, contract)


def ffn_kernel(ids, ins, late, outs, saved, scratch):
    own, core, bias = ins[:3]
    if len(outs) > 4:
        expand, contract, hidden_out, slope_out, keep, send = outs
        parts = ins[3:]
        place_plain(parts, ids[0], expand, 0)
        place_plain(parts, ids[0], contract, 1)
    else:
        expand, contract = ins[3:]
        hidden_out, slope_out, keep, send = outs
    block = own.shape[0]
    for hop, rows, out in ((1, core, send), (0, own, keep)):
        at = slice(hop * block, (hop + 1) * block)
        hidden, slope, part = ffn_rows(rows[...], expand[...], contract[...], bias[...])
        hidden_out[at, :] = hidden
        slope_out[at, :] = slope
        out[...] = part.astype(out.dtype)


def last_norm_kernel(ids, ins, late, outs, saved, scratch):
    keep, from_core, from_x, second, cotangent, rowv = ins
    output, low_out, grad_out, sums = outs
    summed = keep[...] + from_core[...].astype(F32) + from_x[...].astype(F32) + rowv[2:3, :]
    xhat, scale = normalize(second[...] + summed)
    output[...] = (xhat * rowv[7:8, :] + rowv[8:9, :]).astype(BF)
    grad = cotangent[...].astype(F32)
    back = norm_back(grad, xhat, scale, rowv[7:8, :])
    grad_out[...] = back
    low = back.astype(BF)
    low_out[...] = low
    put_sums(sums, low, grad, xhat)


def put_sums(sums, low, grad, normed):
    sums[...] = jnp.zeros_like(sums)
    sums[0:1, :] = col_sum(low.astype(F32))
    sums[1:2, :] = col_sum(grad * normed)
    sums[2:3, :] = col_sum(grad)


def ffn_back_kernel(ids, ins, late, outs, saved, scratch):
    own, core, expand, contract, slope = ins
    pre_out, keep, send = outs
    block = own.shape[0]
    for hop, rows, out in ((1, core, send), (0, own, keep)):
        at = slice(hop * block, (hop + 1) * block)
        grad = (slope[at, :].astype(F32) * nn(rows[...], contract[...])).astype(BF)
        pre_out[at, :] = grad
        out[...] = nt(grad, expand[...]).astype(out.dtype)


def put_blocks(total, place, outs, hops, pack=None):
    if len(outs[0].shape) < 4 - len(outs[1:]):
        if pack is None:
            outs[0][...] = total[...].astype(BF)
        else:
            outs[0][pack] = total[...].astype(BF)
        return
    rows = outs[0].shape[-2]
    level = jnp.right_shift(place, 1)
    for step in range(4):
        for side in range(2):
            index = 2 * (jnp.bitwise_xor(level, step) if hops else step)
            if len(outs) == 2:
                index = index + jnp.bitwise_xor(jnp.bitwise_and(place, 1), side)
                out = outs[side].at[step]
            else:
                index = index + side
                out = outs[0].at[side, step]
            if not isinstance(index, int):
                index = pl.multiple_of(index * rows, rows)
            else:
                index = index * rows
            value = total[pl.ds(index, rows), :].astype(BF)
            if pack is None:
                out[...] = value
            else:
                out[pack] = value


def ffn_grad_kernel(ids, ins, late, outs, saved, scratch):
    rows, grads = ins[:4], ins[4:8]
    hidden_near, hidden_far, pre_near, pre_far = ins[8:]
    (total,) = scratch
    sums, keep = outs
    place = ids[0]
    block = rows[0].shape[0]

    def half(ref, hop):
        return ref[(hop % 2) * block : (hop % 2 + 1) * block, :]

    sums[...] = jnp.zeros_like(sums)
    sums[0:1, :] = col_sum(pre_near[...].astype(F32)) + col_sum(pre_far[...].astype(F32))
    for which, left, near, far in ((1, grads, hidden_near, hidden_far), (0, rows, pre_near, pre_far)):
        for hop in range(4):
            part = tn(left[hop][...], half(far if hop // 2 else near, hop))
            if hop == 0:
                total[...] = part
            else:
                total[...] += part
        put_blocks(total, place, [keep], False, which)


def second_back_kernel(ids, ins, late, outs, saved, scratch):
    keep, from_core, from_x, grad3, rowv = ins
    xhat, scale = late
    low_out, grad_out, sums = outs
    grad = grad3[...] + keep[...] + from_core[...].astype(F32) + from_x[...].astype(F32)
    normed = xhat()[...]
    grad2 = norm_back(grad, normed, scale()[:, 0:1], rowv[5:6, :])
    grad_out[...] = grad2
    low = grad2.astype(BF)
    low_out[...] = low
    put_sums(sums, low, grad, normed)


def first_back_kernel(ids, ins, late, outs, saved, scratch):
    keep, from_core, grad2, rowv = ins
    xhat, scale = late
    low_out, grad_out, sums = outs
    grad = grad2[...] + keep[...] + from_core[...].astype(F32)
    normed = xhat()[...]
    grad1 = norm_back(grad, normed, scale()[:, 0:1], rowv[3:4, :])
    grad_out[...] = grad1
    low = grad1.astype(BF)
    low_out[...] = low
    put_sums(sums, low, grad, normed)


def cross_back_kernel(width, ids, ins, late, outs, saved, scratch):
    own, core = ins
    wide, pair, state, lse = late
    dq_out, dk_out, dv_out, keep, send, bias_sums = outs
    dk_acc, dv_acc = scratch
    block = own.shape[0]
    bias_sums[...] = jnp.zeros_like(bias_sums)
    dk_acc[...] = jnp.zeros_like(dk_acc)
    dv_acc[...] = jnp.zeros_like(dv_acc)
    keys_t = None
    for hop, low in ((1, core), (0, own)):
        at = slice(hop * block, (hop + 1) * block)
        total = jnp.zeros((block, own.shape[1]), F32)
        if keys_t is None:
            keys_t = [transposed(pair()[group, :, :LANES]) for group in range(2)]
        for group in range(2):
            grad_mixed = nn(low[...], wide()[group, :, 3 * LANES :]).astype(BF)

            def add_key(value):
                dk_acc[group] += value

            def add_value(value):
                dv_acc[group] += value

            dq = attend_back(
                state()[group, at, :LANES],
                pair()[group, :, :LANES],
                pair()[group, :, LANES:],
                keys_t[group],
                grad_mixed,
                state()[group, at, LANES:],
                lambda head: lse()[group, head : head + 1, at],
                width,
                None,
                add_key,
                add_value,
            )
            dq_low = (dq.astype(BF).astype(F32) * 0.125).astype(BF)
            dq_out[group, at, :] = dq_low
            bias_sums[group, 0:1, :] += col_sum(dq_low.astype(F32))
            total = total + nt(dq_low, wide()[group, :, :LANES])
        if hop:
            send[...] = total.astype(BF)
        else:
            keep[...] = total
    for group in range(2):
        dk_out[group] = dk_acc[group].astype(BF)
        dv_low = dv_acc[group].astype(BF)
        dv_out[group] = dv_low
        bias_sums[group, 1:2, :] = col_sum(dv_low.astype(F32))


def cross_grad_kernel(width, ids, ins, late, outs, saved, scratch):
    dq, dk, dv, low_two, low_two_core, low1, low1_core = ins
    wide, state, memory = late
    (total,) = scratch
    mem_keep, mem_x, mem_send = outs[:3]
    place, rank = ids[0], ids[1]
    block = mem_keep.shape[0]
    rows = low1.shape[0]
    for group in range(2):
        total[:, 3 * width :] = (
            tn(low_two[...], state()[group, :rows, LANES:])
            + tn(low_two_core[...], state()[group, rows:, LANES:])
        )[:, :width]
        total[:, :width] = (
            tn(low1[...], dq[group, :rows, :]) + tn(low1_core[...], dq[group, rows:, :])
        )[:, :width]
        total[:, width : 2 * width] = tn(memory()[...], dk[group])[:, :width]
        total[:, 2 * width : 3 * width] = tn(memory()[...], dv[group])[:, :width]
        put_blocks(total, place, outs[3:], True, group)
    for hop in (1, 3, 2, 0):
        start = block_start(rank, block, 4, hop)
        part = jnp.zeros((block, wide().shape[1]), F32)
        for group in range(2):
            part = part + nt(dk[group, pl.ds(start, block), :], wide()[group, :, LANES : 2 * LANES])
            part = part + nt(
                dv[group, pl.ds(start, block), :], wide()[group, :, 2 * LANES : 3 * LANES]
            )
        if hop == 0:
            mem_keep[...] = part
        elif hop == 2:
            mem_x[...] = part
        else:
            mem_send[hop // 2] = part.astype(BF)


def self_back_kernel(width, ids, ins, late, outs, saved, scratch):
    grads = ins
    wide, state, lse, target = late
    low, total, dk_acc, dv_acc = scratch
    three, bias_sums = outs[:2]
    keeps = outs[2:]
    place, rank = ids[0], ids[1]
    length = low.shape[0]
    block = length // 4
    place_plain(grads, rank, low)
    grad_mixed = nn(low[...], wide()[:, 3 * LANES :]).astype(BF)
    q_in, k_in, v_in, mixed = (state().at[:, i * LANES : (i + 1) * LANES] for i in range(4))
    keys_t = transposed(k_in[...])
    dk_acc[...] = jnp.zeros_like(dk_acc)
    dv_acc[...] = jnp.zeros_like(dv_acc)
    bias_sums[...] = jnp.zeros_like(bias_sums)
    for index in range(4):
        start, stop = index * block, (index + 1) * block

        def add_key(value):
            dk_acc[:stop, :] += value

        def add_value(value):
            dv_acc[:stop, :] += value

        dq = attend_back(
            q_in[start:stop, :],
            k_in[:stop, :],
            v_in[:stop, :],
            keys_t[:, :stop],
            grad_mixed[start:stop],
            mixed[start:stop, :],
            lambda head: lse()[head : head + 1, start:stop],
            width,
            start,
            add_key,
            add_value,
        )
        three[start:stop, :LANES] = (dq.astype(BF).astype(F32) * 0.125).astype(BF)
    three[:, LANES : 2 * LANES] = dk_acc[...].astype(BF)
    three[:, 2 * LANES :] = dv_acc[...].astype(BF)
    bias_sums[0:1, :] = col_sum(three[:, :LANES].astype(F32))
    bias_sums[1:2, :] = col_sum(three[:, 2 * LANES :].astype(F32))
    part = tn(target()[...], three[...])
    for group in range(3):
        total[:, group * width : (group + 1) * width] = part[
            :, group * LANES : group * LANES + width
        ]
    total[:, 3 * width :] = tn(low[...], mixed[...])[:, :width]
    put_blocks(total, place, keeps, True)


def target_kernel(ids, ins, late, outs, saved, scratch):
    (three,) = ins
    (wide,) = late
    keep, keep_x, send = outs
    rank = ids[1]
    block = keep.shape[0]
    for hop in (3, 1, 2, 0):
        start = block_start(rank, block, 4, hop)
        part = nt(three[pl.ds(start, block), :], wide()[:, : 3 * LANES])
        if hop == 0:
            keep[...] = part
        elif hop == 2:
            keep_x[...] = part
        else:
            send[hop // 2] = part.astype(BF)


def join_kernel(ids, ins, late, outs, saved, scratch):
    rank = ids[1]
    block = ins[0].shape[0]
    for hop, part in enumerate(ins):
        outs[0][pl.ds(block_start(rank, block, 4, hop), block), :] = part[...].astype(outs[0].dtype)


def adam(weight, gradient, moment, square, rate, clip_scale):
    clipped = gradient * clip_scale
    new_moment = BETA_ONE * moment + (1.0 - BETA_ONE) * clipped
    new_square = BETA_TWO * square + (1.0 - BETA_TWO) * clipped * clipped
    fixed_moment = new_moment / (1.0 - BETA_ONE**STEP)
    fixed_square = new_square / (1.0 - BETA_TWO**STEP)
    new_weight = weight - rate * (
        fixed_moment / (jnp.sqrt(fixed_square) + ADAM_EPS) + DECAY * weight
    )
    return (new_weight, new_moment, new_square)


def adam_kernel(width, ids, ins, late, outs, saved, scratch):
    squares, own, cross, expand, contract, small = ins[:6]
    leaves = [ins[6 + 3 * i : 9 + 3 * i] for i in range(7)]
    norm = jnp.sqrt(squares[0:1, 0:1])
    outs[0][...] = jnp.broadcast_to(norm, outs[0].shape)
    scale = jnp.minimum(1.0, MAX_NORM / (norm + 1e-06))

    def update(leaf, index, at, gradient, rate):
        weight, moment, square = (ref[at] for ref in leaf)
        new = adam(weight, gradient, moment, square, rate, scale)
        first = 1 + 4 * index if index < 4 else 17 + 3 * (index - 4)
        for i in range(3):
            outs[first + i][at] = new[i]
        if index < 4:
            outs[first + 3][at] = new[0].astype(BF)

    everything = (slice(None), slice(None))
    for half, pack in enumerate((own, cross)):
        for i in range(3):
            part = pack[:, i * width : (i + 1) * width]
            update(leaves[0], 0, 3 * half + i, part, RATE_MATRIX)
        update(leaves[1], 1, half, pack[:, 3 * width :].T, RATE_MATRIX)
    update(leaves[2], 2, everything, expand[...], RATE_MATRIX)
    update(leaves[3], 3, everything, contract[...], RATE_MATRIX)
    for i in range(4):
        at = (slice(i, i + 1), slice(None))
        update(leaves[4], 4, at, small[9:10, i * width : (i + 1) * width], RATE_VECTOR)
    update(leaves[5], 5, everything, small[10:11, :], RATE_VECTOR)
    update(leaves[6], 6, everything, small[0:9, :], RATE_VECTOR)


def local(
    data_size,
    tensor_size,
    target,
    memory,
    target_segments,
    memory_segments,
    cotangent,
    input_weights,
    input_moment,
    input_square,
    output_weights,
    output_moment,
    output_square,
    expand_weights,
    expand_moment,
    expand_square,
    contract_weights,
    contract_moment,
    contract_square,
    head_biases,
    head_moment,
    head_square,
    hidden_biases,
    hidden_moment,
    hidden_square,
    row_vectors,
    row_moment,
    row_square,
):
    length, model = target.shape[1:]
    mem_length = memory.shape[1]
    width = head_biases.shape[1]
    block = length // tensor_size
    mem_block = mem_length // tensor_size
    share = model // data_size
    direct = data_size == 8 and share % 16 == 0
    place = lax.axis_index("dp")
    rank = lax.axis_index("tensor")
    ids = jnp.stack([place, rank]).astype(jnp.int32)
    target_rows = target.reshape(length, model)
    memory_rows = memory.reshape(mem_length, model)
    cotangent_rows = cotangent.reshape(length, model)
    target_seg = target_segments.reshape(length, 1)
    memory_seg = memory_segments.reshape(mem_length, 1)
    rowv = jnp.pad(row_vectors, ((0, 7), (0, 0)))
    bias = jnp.pad(head_biases, ((0, 4), (0, LANES - width)))

    def to_tensor(value, hop):
        return lax.ppermute(value, "tensor", [(i, i ^ hop) for i in range(tensor_size)])

    def to_data(value, hop):
        return lax.ppermute(value, "dp", [(i, i ^ hop) for i in range(data_size)])

    def over_z(value):
        groups = [list(range(side, data_size, 2)) for side in range(2)]
        return lax.all_to_all(value, "dp", 0, 0, axis_index_groups=groups, tiled=True)

    def gather_plain(value):
        return [lax.all_gather(value, "dp", axis=value.ndim - 2, tiled=True)]

    def spread(value):
        return over_z(jnp.broadcast_to(value[None], (4,) + value.shape))

    def over_y(value):
        groups = [[side, side + 1] for side in range(0, data_size, 2)]
        return lax.all_to_all(value, "dp", 0, 0, axis_index_groups=groups, tiled=True)

    def added(received):
        return (received[0].astype(F32) + received[1].astype(F32)).astype(BF)

    def hops_z(value):
        return [value[0]] + [to_data(value[hop], 2 * hop) for hop in (1, 2, 3)]

    def total_of(received):
        first, second, third, fourth = (part.astype(F32) for part in received)
        return (first + second) + (third + fourth)

    def scatter_plain(value):
        return lax.psum_scatter(
            value, "dp", scatter_dimension=value.ndim - 2, tiled=True
        ).astype(F32)

    def sum_data(value):
        if not direct:
            return lax.psum(value, "dp")
        value = value + to_data(value, 1)
        got = [to_data(value, hop) for hop in (2, 4, 6)]
        return (value + got[0]) + (got[1] + got[2])

    def join(own, far, dtype):
        core = to_tensor(own, 1)
        diag = to_tensor(far, 1)
        rows = own.shape[0] * 4
        return call(
            join_kernel, ids, [own, core, far, diag], [], [SDS((rows, model), dtype)], [], name="join"
        )[0]

    def sum_rows(keep_x, send_x):
        return (keep_x + send_x.astype(F32)).astype(BF)

    self_pack = jnp.concatenate(
        [input_weights[0], input_weights[1], input_weights[2], output_weights[0].T], axis=1
    ).astype(BF)
    cross_pack = jnp.concatenate(
        [input_weights[3], input_weights[4], input_weights[5], output_weights[1].T], axis=1
    ).astype(BF)
    cross_far = to_tensor(cross_pack, 2)
    bias_far = to_tensor(bias, 2)
    target_own = lax.dynamic_slice_in_dim(target_rows, rank * block, block, 0)
    cotangent_own = lax.dynamic_slice_in_dim(cotangent_rows, rank * block, block, 0)
    seg_near = jnp.concatenate(
        [
            lax.dynamic_slice_in_dim(target_seg, (rank ^ hop) * block, block, 0)
            for hop in range(2)
        ]
    )
    cross_pair = jnp.stack([cross_pack, cross_far])
    ffn_pair = jnp.stack([expand_weights.astype(BF), contract_weights.T.astype(BF)])
    if direct:
        self_z = [to_data(self_pack, hop) for hop in (2, 4, 6)]
        self_parts = [self_pack, to_data(self_pack, 1)]
        for part in self_z:
            self_parts += [part, to_data(part, 1)]
        cross_parts = [spread(cross_pair)]
        cross_parts.append(to_data(cross_parts[0], 1))
    else:
        self_parts, cross_parts = gather_plain(self_pack), gather_plain(cross_pair)
    cross_bias = jnp.stack([bias, bias_far])

    quarter = SDS((block, model), F32)
    quarter_low = SDS((block, model), BF)
    pair_low = SDS((2, block, model), BF)
    column = SDS((block, 128), F32)
    sums_shape = SDS((8, model), F32)
    padded = 4 * LANES

    (keep, keep_x, send, wide_self, state_self, lse_self) = call(
        partial(self_kernel, width),
        ids,
        [target_rows, target_seg, bias, *self_parts],
        [],
        [quarter, quarter, pair_low],
        [SDS((model, padded), BF), SDS((length, padded), BF), SDS((8, length), F32)],
        flops=2 * length * model * padded + 8 * length * length * LANES,
        name="self_forward",
    )
    from_core = to_tensor(send, 1)
    to_far = sum_rows(keep_x, from_core[1])
    from_x = to_tensor(to_far, 2)
    if direct:
        ffn_parts = [spread(after(ffn_pair, to_far))]
        ffn_parts.append(to_data(ffn_parts[0], 1))
    else:
        ffn_parts = gather_plain(ffn_pair)

    mem_rows = SDS((2, mem_length, LANES), BF)
    wide_cross, kv_cross = call(
        partial(memory_kernel, width),
        ids,
        [memory_rows, memory_seg, cross_bias, *cross_parts],
        [],
        [],
        [SDS((2, model, padded), BF), SDS((2, mem_length, 2 * LANES), BF)],
        flops=8 * mem_length * model * LANES,
        name="memory_rows",
    )
    low1, first, xhat1, scale1 = call(
        first_norm_kernel,
        ids,
        [keep, from_core, from_x, target_own, rowv],
        [],
        [quarter_low, quarter],
        [quarter, column],
        name="first_norm",
    )
    low1_core = to_tensor(low1, 1)
    pair_rows = SDS((2, 2 * block, LANES), BF)
    keep, send, state_cross, lse_cross = call(
        partial(cross_kernel, width),
        ids,
        [low1, low1_core, seg_near, cross_bias],
        [wide_cross, kv_cross],
        [quarter, quarter_low],
        [SDS((2, 2 * block, 2 * LANES), BF), SDS((2, 8, 2 * block), F32)],
        flops=16 * block * model * LANES + 48 * block * mem_length * LANES,
        name="cross_forward",
    )
    low2, second, xhat2, scale2 = call(
        second_norm_kernel,
        ids,
        [keep, to_tensor(send, 1), first, rowv],
        [],
        [quarter_low, quarter],
        [quarter, column],
        name="second_norm",
    )

    low2_x = to_tensor(low2, 2)
    low2_core = to_tensor(low2, 1)
    hidden_row = hidden_biases.reshape(1, -1)
    units = hidden_row.shape[1]
    half_units = SDS((2 * block, units), BF)
    ffn_flops = 8 * block * model * units
    expand_all, contract_all, hidden_near, slope_near, keep, send = call(
        ffn_kernel,
        ids,
        [low2, low2_core, hidden_row, *ffn_parts],
        [],
        [SDS((model, units), BF)] * 2 + [half_units, half_units, quarter, quarter_low],
        [],
        flops=ffn_flops,
        name="ffn_near",
    )
    from_core = to_tensor(send, 1)
    low2_diag = to_tensor(low2_x, 1)
    hidden_far, slope_far, keep_x, send = call(
        ffn_kernel,
        ids,
        [low2_x, low2_diag, hidden_row, expand_all, contract_all],
        [],
        [half_units, half_units, quarter, quarter_low],
        [],
        flops=ffn_flops,
        name="ffn_far",
    )
    from_x = to_tensor(sum_rows(keep_x, to_tensor(send, 1)), 2)
    out_own, low3, grad3, sums3 = call(
        last_norm_kernel,
        ids,
        [keep, from_core, from_x, second, cotangent_own, rowv],
        [],
        [quarter_low, quarter_low, quarter, sums_shape],
        [],
        name="last_norm",
    )

    low3_x = to_tensor(low3, 2)
    low3_core = to_tensor(low3, 1)
    pre_near, keep, send = call(
        ffn_back_kernel,
        ids,
        [low3, low3_core, expand_all, contract_all, slope_near],
        [],
        [half_units, quarter, quarter_low],
        [],
        flops=ffn_flops,
        name="ffn_back_near",
    )
    from_core = to_tensor(send, 1)
    low3_diag = to_tensor(low3_x, 1)
    pre_far, keep_x, send = call(
        ffn_back_kernel,
        ids,
        [low3_x, low3_diag, expand_all, contract_all, slope_far],
        [],
        [half_units, quarter, quarter_low],
        [],
        flops=ffn_flops,
        name="ffn_back_far",
    )
    to_far = sum_rows(keep_x, to_tensor(send, 1))
    from_x = to_tensor(to_far, 2)
    blocks = [SDS((4, share, model), BF)] * 2 if direct else [SDS((model, model), BF)]
    pair = SDS((2, 4, 2, share, model), BF) if direct else SDS((2, model, model), BF)
    ffn_outs = call(
        ffn_grad_kernel,
        ids,
        [after(low2, to_far), low2_core, low2_x, low2_diag, low3, low3_core, low3_x, low3_diag]
        + [hidden_near, hidden_far, pre_near, pre_far],
        [],
        [SDS((8, units), F32)] + [pair],
        [],
        [pltpu.VMEM((model, units), F32)],
        flops=2 * ffn_flops,
        name="ffn_grad",
    )
    hidden_sums = ffn_outs[0]
    ffn_along = over_y(ffn_outs[1]) if direct else None

    low_two, grad2, sums2 = call(
        second_back_kernel,
        ids,
        [after(keep, ffn_outs[1]), from_core, from_x, grad3, rowv],
        [xhat2, scale2],
        [quarter_low, quarter, sums_shape],
        [],
        name="second_back",
    )
    low_two_core = to_tensor(low_two, 1)
    output_far = to_tensor(after(out_own, low_two), 2)
    dq, dk, dv, keep, send, bias_sums = call(
        partial(cross_back_kernel, width),
        ids,
        [low_two, low_two_core],
        [wide_cross, kv_cross, state_cross, lse_cross],
        [pair_rows, mem_rows, mem_rows, quarter, quarter_low, SDS((2, 8, LANES), F32)],
        [],
        [pltpu.VMEM((2, mem_length, LANES), F32)] * 2,
        flops=16 * block * model * LANES + 120 * block * mem_length * LANES,
        name="cross_back",
    )
    mem_quarter = SDS((mem_block, model), F32)
    cross_outs = call(
        partial(cross_grad_kernel, width),
        ids,
        [dq, dk, dv, low_two, low_two_core, low1, low1_core],
        [wide_cross, state_cross, memory_rows],
        [mem_quarter, mem_quarter, SDS((2, mem_block, model), BF)]
        + ([SDS((4, 2, share, model), BF)] * 2 if direct else [pair]),
        [],
        [pltpu.VMEM((model, model), F32)],
        flops=24 * mem_length * model * LANES,
        name="cross_grad",
    )
    mem_keep, mem_x, mem_send = cross_outs[:3]
    cross_along = to_data(cross_outs[4], 1) if direct else None

    low_one, grad1, sums1 = call(
        first_back_kernel,
        ids,
        [after(keep, cross_outs[0]), to_tensor(after(send, output_far), 1), grad2, rowv],
        [xhat1, scale1],
        [quarter_low, quarter, sums_shape],
        [],
        name="first_back",
    )
    low_one_x = to_tensor(low_one, 2)
    low_one_core = to_tensor(low_one, 1)
    if direct:
        ffn_received = over_z(added(ffn_along))
    low_one_diag = to_tensor(low_one_x, 1)

    back_outs = call(
        partial(self_back_kernel, width),
        ids,
        [low_one, low_one_core, low_one_x, low_one_diag],
        [wide_self, state_self, lse_self, target_rows],
        [SDS((length, 3 * LANES), BF), SDS((8, LANES), F32)] + blocks,
        [],
        [pltpu.VMEM((length, model), BF), pltpu.VMEM((model, model), F32)]
        + [pltpu.VMEM((length, LANES), F32)] * 2,
        flops=4 * length * model * padded + 20 * length * length * LANES,
        name="self_back",
    )
    three, self_sums, keep_self = back_outs[:3]
    if direct:
        self_along = to_data(back_outs[3], 1)
        late_rows = after(jnp.stack(
            [sums1[0], sums2[0], sums3[0], sums1[1], sums1[2], sums2[1], sums2[2], sums3[1], sums3[2]]
        ), self_along)
        cross_received = hops_z(added((cross_outs[3], cross_along)))
        self_received = hops_z(added((keep_self, self_along)))
        ffn_share = total_of(ffn_received)
        cross_both = total_of(cross_received)
        self_share = total_of(self_received)
    else:
        ffn_share = scatter_plain(ffn_outs[1])
        cross_both = scatter_plain(cross_outs[3])
        self_share = scatter_plain(keep_self)
        late_rows = jnp.stack(
            [sums1[0], sums2[0], sums3[0], sums1[1], sums1[2], sums2[1], sums2[2], sums3[1], sums3[2]]
        )
    cross_share = cross_both[0] + to_tensor(cross_both[1].astype(BF), 2).astype(F32)
    expand_share, contract_share = ffn_share[0], ffn_share[1]

    keep, keep_x, send = call(
        target_kernel,
        ids,
        [three],
        [wide_self],
        [quarter, quarter, pair_low],
        [],
        flops=6 * length * model * LANES,
        name="target_grad",
    )
    from_core = to_tensor(send, 1)
    from_x = to_tensor(sum_rows(keep_x, from_core[1]), 2)
    target_sum = (grad1 + keep + from_core[0].astype(F32) + from_x.astype(F32)).astype(BF)
    from_core = to_tensor(after(mem_send, three), 1)
    from_x = to_tensor(sum_rows(mem_x, from_core[1]), 2)
    memory_sum = (mem_keep + from_core[0].astype(F32) + from_x.astype(F32)).astype(BF)

    output = join(out_own, output_far, BF)
    memory_far = to_tensor(memory_sum, 2)
    memory_grad = join(memory_sum, memory_far, F32)
    target_far = to_tensor(target_sum, 2)
    target_grad = join(target_sum, target_far, F32)

    row_part = late_rows
    row_part = row_part + to_tensor(row_part, 1)
    row_part = row_part + to_tensor(row_part, 2)
    cross_sums = bias_sums[:, :2, :width]
    near = cross_sums[0] + to_tensor(cross_sums[1], 2)
    head_part = jnp.concatenate([self_sums[:2, :width], near], axis=0)
    small = sum_data(
        jnp.concatenate([row_part, head_part.reshape(1, -1), hidden_sums[:1]], axis=0)
    )
    row_grad = small[:9]
    head_grad = small[9].reshape(4, width)
    hidden_grad = small[10]

    own_squares = (
        jnp.sum(self_share * self_share)
        + jnp.sum(cross_share * cross_share)
        + jnp.sum(expand_share * expand_share)
        + jnp.sum(contract_share * contract_share)
    )
    shared_squares = (
        jnp.sum(head_grad * head_grad) + jnp.sum(hidden_grad * hidden_grad)
    ) / data_size
    common_squares = jnp.sum(row_grad * row_grad) / (data_size * tensor_size)
    squares = (own_squares + shared_squares + common_squares).reshape(1, 1)
    squares = after(squares, target_far, memory_far)
    squares = squares + to_tensor(squares, 1)
    squares = squares + to_tensor(squares, 2)
    squares = sum_data(after(squares, target_grad))
    hidden = [value.reshape(1, -1) for value in (hidden_biases, hidden_moment, hidden_square)]
    leaves = [input_weights, input_moment, input_square, output_weights, output_moment]
    leaves += [output_square, expand_weights, expand_moment, expand_square]
    leaves += [value.T for value in (contract_weights, contract_moment, contract_square)]
    leaves += [head_biases, head_moment, head_square, *hidden]
    leaves += [row_vectors, row_moment, row_square]
    shapes = [SDS((1, 1), F32)]
    for i in range(7):
        shapes += [SDS(leaf.shape, F32) for leaf in leaves[3 * i : 3 * i + 3]]
        if i < 4:
            shapes.append(SDS(leaves[3 * i].shape, BF))
    new = call(
        partial(adam_kernel, width),
        ids,
        [squares, self_share, cross_share, expand_share, contract_share, small, *leaves],
        [],
        shapes,
        [],
        name="adam",
    )
    return (
        output.reshape(target.shape),
        target_grad.reshape(target.shape),
        memory_grad.reshape(memory.shape),
        new[0][0, 0],
        *new[1:13],
        *(value.T for value in new[13:17]),
        *new[17:20],
        *(value.reshape(-1) for value in new[20:23]),
        *new[23:],
    )


def solution(mesh):
    rows = P("dp", None, None)
    in_matrix = P(None, "dp", "tensor")
    out_matrix = P(None, "tensor", "dp")
    return jax.shard_map(
        partial(local, mesh.shape["dp"], mesh.shape["tensor"]),
        mesh=mesh,
        in_specs=(rows, rows, P("dp", None), P("dp", None), rows)
        + (in_matrix,) * 3
        + (out_matrix,) * 3
        + (P("dp", "tensor"),) * 3
        + (P("tensor", "dp"),) * 3
        + (P(None, "tensor"),) * 3
        + (P("tensor"),) * 3
        + (P(),) * 3,
        out_specs=(rows, rows, rows, P())
        + (in_matrix,) * 4
        + (out_matrix,) * 4
        + (P("dp", "tensor"),) * 4
        + (P("tensor", "dp"),) * 4
        + (P(None, "tensor"),) * 3
        + (P("tensor"),) * 3
        + (P(),) * 3,
        check_vma=False,
    )
```
